128 devices in a mesh: section: 2 (over z_lo), peer: 64 (over x, y, z_hi, core).
Axes of the slice: x: 4, y: 4, z: 4 (z_hi: 2, z_lo: 2; z = z_hi * 2 + z_lo), core: 2. Of those that a mesh axis runs over, the one named last changes fastest.
Arguments:
- batch_ends: bfloat16 [2, 8192, 5120], P('section', 'peer'), may hold values from -6 to 6
- wiring: int32 [64], replicated, may hold values from 0 to 63, as said below
- down_proj: bfloat16 [2, 64, 5120, 256], P('section', 'peer'), may hold values from -0.078125 to 0.078125
- up_proj: bfloat16 [2, 64, 256, 5120], P('section', 'peer'), may hold values from -0.375 to 0.375
- norm_gain: bfloat16 [2, 64, 5120], P('section', 'peer'), may hold values from 0.099609375 to 1.8984375
Outputs:
- ends_grad: bfloat16 [2, 8192, 5120], P('section', 'peer')
- down_grad: float32 [2, 5120, 256], P('section', 'peer')
- up_grad: float32 [2, 256, 5120], P('section', 'peer')
The draws below stay inside these ranges and needn't reach their ends.
Inputs may be any that keep to these rules, and one draw needn't show every extreme that they name: `wiring`: no value is named by more than 2 entries; a quarter of the peers are named by exactly 2 entries, half by one, a quarter by none.
All inputs are finite; a program needn't handle non-finite values.
Results may differ from the reference program's by a relative error of at most 0.0067.
Values may be sent and summed in bfloat16 or wider, within the bound.
A program may use at most 128 MiB of HBM per device.

```python
import math
import jax
import jax.numpy as jnp
from jax import lax

D = 5120
R = 256
TOK_DEV = 128
TOKENS = 8192
N_PEER = 64


def draw_wiring(key, part):
    key = jax.random.fold_in(key, 11)
    first_key, second_key = jax.random.split(key)
    order = jax.random.permutation(first_key, N_PEER)
    quarter = N_PEER // 4
    picks = jnp.concatenate([order[:quarter], order[:quarter], order[quarter:3 * quarter]])
    return jax.random.permutation(second_key, picks).astype(jnp.int32)


def level_of(key, extent, shards, least, largest):
    level, own = 1.0, jax.random.fold_in(key, 6)
    for axis_at, parts in shards:
        steps = jnp.exp(jax.random.uniform(jax.random.fold_in(own, axis_at), (parts,), jnp.float32, least / len(shards), largest / len(shards)))
        level = level * jnp.repeat(steps, extent[axis_at] // parts).reshape([-1 if axis == axis_at else 1 for axis in range(len(extent))])
    return level


def bell_draw(key, extent, width, most, pieces=(), kind=jnp.bfloat16):
    values = jax.random.normal(key, extent, jnp.float32) * width
    if len(pieces) > 0:
        values = level_of(key, extent, pieces, -0.22, 0.18) * values
    return jnp.clip(values, min=-most, max=most).astype(kind)


def setup_inputs(seed: int = 0) -> dict:
    key_of = jax.random.split(jax.random.key(seed), 6)
    batch_ends = bell_draw(key_of[0], (2, TOKENS, D), 1.0, 6.0, ((0, 2), (1, 64)))
    wiring = draw_wiring(jax.random.fold_in(key_of[5], 71), 0)
    down_proj = bell_draw(key_of[2], (2, N_PEER, D, R), D ** -0.5, 0.078125, ((0, 2), (1, 64)))
    up_proj = bell_draw(key_of[3], (2, N_PEER, R, D), R ** -0.5, 0.375, ((0, 2), (1, 64)))
    norm_gain = jnp.clip(1.0 + 0.18 * jax.random.normal(key_of[4], (2, N_PEER, D), jnp.float32), 0.099609375, 1.8984375).astype(jnp.bfloat16)
    return dict(batch_ends=batch_ends, wiring=wiring, down_proj=down_proj, up_proj=up_proj, norm_gain=norm_gain)


def contract_rows(left, right):
    return lax.dot_general(left, right, (((0,), (0,)), ((), ())), preferred_element_type=jnp.float32)

def contract_cols(left, right):
    return lax.dot_general(left, right, (((1,), (1,)), ((), ())), preferred_element_type=jnp.float32)

def section_forward(tok_rows, norm_scale, down_matrix, up_matrix):
    values = tok_rows.astype(jnp.float32)
    inverse = lax.rsqrt(lax.optimization_barrier(jnp.mean(values * values, axis=-1, keepdims=True)) + 1e-06)
    normed = (values * inverse * norm_scale.astype(jnp.float32)).astype(jnp.bfloat16)
    activation = jnp.dot(normed, down_matrix, preferred_element_type=jnp.float32)
    squashed = jax.nn.silu(activation).astype(jnp.bfloat16)
    result = (values + jnp.dot(squashed, up_matrix, preferred_element_type=jnp.float32)).astype(jnp.bfloat16)
    return (result, (normed, activation, squashed, inverse))

def section_backward(tok_rows, cotangent, norm_scale, down_matrix, up_matrix, saved):
    normed, activation, squashed, inverse = saved
    grad_up = contract_rows(squashed, cotangent)
    grad_squash = contract_cols(cotangent, up_matrix)
    sigmoid = jax.nn.sigmoid(activation)
    grad_act = (grad_squash * sigmoid * (1.0 + activation * (1.0 - sigmoid))).astype(jnp.bfloat16)
    grad_down = contract_rows(normed, grad_act)
    grad_normed = contract_cols(grad_act, down_matrix) * norm_scale.astype(jnp.float32)
    values = tok_rows.astype(jnp.float32)
    grad_values = inverse * grad_normed - values * inverse ** 3 * lax.optimization_barrier(jnp.mean(values * grad_normed, axis=-1, keepdims=True))
    grad_rows = (cotangent.astype(jnp.float32) + grad_values).astype(jnp.bfloat16)
    return (grad_rows, grad_down, grad_up)

def reference(batch_ends, wiring, down_proj, up_proj, norm_gain):
    inputs = batch_ends[0].reshape(N_PEER, TOK_DEV, D)
    cotangents = batch_ends[1].reshape(N_PEER, TOK_DEV, D)

    def advance(totals, item):
        source, first_rows, final_cot = item
        target = wiring[source]
        hidden, saved_first = section_forward(first_rows, norm_gain[0, source], down_proj[0, source], up_proj[0, source])
        ignored, saved_second = section_forward(hidden, norm_gain[1, target], down_proj[1, target], up_proj[1, target])
        boundary, second_down, second_up = section_backward(hidden, final_cot, norm_gain[1, target], down_proj[1, target], up_proj[1, target], saved_second)
        start_grad, first_down, first_up = section_backward(first_rows, boundary, norm_gain[0, source], down_proj[0, source], up_proj[0, source], saved_first)
        totals = (totals[0] + first_down, totals[1] + first_up, totals[2] + second_down, totals[3] + second_up)
        return (totals, (start_grad, boundary))
    zero_down = jnp.zeros((D, R), jnp.float32)
    zero_up = jnp.zeros((R, D), jnp.float32)
    sources = jnp.arange(N_PEER, dtype=jnp.int32)
    totals, outputs = lax.scan(advance, (zero_down, zero_up, zero_down, zero_up), (sources, inputs, cotangents))
    factor = 1.0 / math.sqrt(TOKENS)
    ends_grad = jnp.stack([outputs[0].reshape(TOKENS, D), outputs[1].reshape(TOKENS, D)])
    down_grad = jnp.stack([totals[0], totals[2]]) * factor
    up_grad = jnp.stack([totals[1], totals[3]]) * factor
    return (ends_grad, down_grad, up_grad)
```

```python
import functools
import math

import jax
import jax.numpy as jnp
from jax import lax
from jax.experimental import pallas as pl
from jax.experimental.pallas import tpu as pltpu
from jax.sharding import PartitionSpec as P

N = 64
ROWS = 16
COLS = 640
WAYS = 8
TOK, WIDTH, RANK = 128, 5120, 256
BF, F32 = jnp.bfloat16, jnp.float32
MESH = pl.DeviceIdType.MESH

(ENDS, COT, HID, GAIN, NORM, SQ0, BACK, SQ1, GA1, BND0, BND1, GA0, DOWN, UPA, UPA1, UPB, CLASSES) = range(17)


def target(p, k):
    a = lax.rem(lax.rem(k, 4) + 2 * lax.rem(p, 2), 4)
    b = lax.rem(k // 4, 4)
    x = lax.rem(p // 16 + a, 4)
    y = lax.rem(lax.rem(p // 4, 4) + a + b, 4)
    z = lax.rem(lax.rem(p // 2, 2) + lax.rem(k // 16, 2) + a, 2)
    core = lax.rem(lax.rem(p, 2) + k // 32 + a // 2, 2)
    return x * 16 + y * 4 + z * 2 + core


def nn(left, right):
    return jnp.dot(left, right, preferred_element_type=F32)


def nt(left, right):
    return lax.dot_general(left, right, (((1,), (1,)), ((), ())), preferred_element_type=F32)


def tn(left, right):
    return lax.dot_general(left, right, (((0,), (0,)), ((), ())), preferred_element_type=F32)


def loop(count, body):
    def step(k, carry):
        body(k)
        return carry

    lax.fori_loop(0, count, step, 0)


def tile(t):
    return pl.ds(pl.multiple_of(t * COLS, 128), COLS)


def strip(i):
    return pl.ds(pl.multiple_of(i * ROWS, ROWS), ROWS)


def step_kernel(
    from_ref, back_ref, own_ref, down_ref, up_ref, gain_ref,
    ends_ref, dgrad_ref, ugrad_ref,
    pieces, picked, hid, normed, hid_in, cot_in, gain_out, gain_in, norm_in,
    sq_out, sq0_in, sq_slots, ga_slots, back_in, sq1_in, ga1_in, bnd_pick, bnd, sq_pick,
    ga_out, ga0_in, act_ref, gsq_ref, inv_ref, part_d, part_u, part_u1, acc_d, acc_u, slab, slab_in,
    send, recv,
):
    s = lax.axis_index("section")
    p = lax.axis_index("peer")
    first, second = s == 0, s == 1
    row_group, col_group = p // WAYS, lax.rem(p, WAYS)
    my_rows, my_cols = strip(row_group), tile(col_group)

    def push(src, dst, kind, section, peer):
        pltpu.make_async_remote_copy(
            src_ref=src, dst_ref=dst, send_sem=send.at[kind], recv_sem=recv.at[kind],
            device_id={"section": section, "peer": peer}, device_id_type=MESH,
        ).start()

    def push_or_keep(src, dst, kind, peer):
        @pl.when(peer != p)
        def _():
            push(src, dst, kind, s, peer)

        @pl.when(peer == p)
        def _():
            pltpu.make_async_copy(src, dst, recv.at[kind]).start()

    def arrived(kind, ref):
        pltpu.make_async_copy(ref, ref, recv.at[kind]).wait()

    def left(kind, ref):
        pltpu.make_async_copy(ref, ref, send.at[kind]).wait()

    barrier = pltpu.get_barrier_semaphore()

    def greet(k):
        t = lax.rem(p + k, N)
        pl.semaphore_signal(barrier, inc=1, device_id={"section": 1 - s, "peer": t}, device_id_type=MESH)

        @pl.when(k > 0)
        def _():
            pl.semaphore_signal(barrier, inc=1, device_id={"section": s, "peer": t}, device_id_type=MESH)

    loop(N, greet)

    def all_here():
        pl.semaphore_wait(barrier, 2 * N - 1)

    def choose_and_send(kind, dst_ref):
        def one(k):
            q = target(p, k)
            picked[q, 0] = pieces[from_ref[0, q]]
            picked[q, 1] = pieces[from_ref[1, q]]
            dst = dst_ref.at[:, my_rows, my_cols]
            if kind == HID:
                push_or_keep(picked.at[q], dst, kind, q)
            else:
                push(picked.at[q], dst, kind, 1, q)

        loop(N, one)

    def middle(act, gsq):
        sig = jax.nn.sigmoid(act)
        squashed = (act * sig).astype(BF)
        ga = (gsq * sig * (1.0 + act * (1.0 - sig))).astype(BF)
        return squashed, ga

    def partial(out, left_ref, right_ref):
        out[...] = jnp.zeros_like(out)

        def some(t):
            rows = pl.ds(t * 16, 16)
            a = left_ref[rows].reshape(16 * ROWS, left_ref.shape[2])
            b = right_ref[rows].reshape(16 * ROWS, right_ref.shape[2])
            out[...] += tn(a, b)

        loop(4, some)

    def send_up(part, kind, section):
        def one(i):
            src = part.at[pl.ds(pl.multiple_of(i * 32, 32), 32)]
            dst = acc_u.at[row_group]
            peer = i * WAYS + col_group
            if kind == UPA:
                push_or_keep(src, dst, kind, peer)
            else:
                push(src, dst, kind, section, peer)

        loop(WAYS, one)

    def send_down():
        def one(r):
            src = part_d.at[pl.ds(pl.multiple_of(r * 80, 16), 80)]
            push_or_keep(src, acc_d.at[row_group], DOWN, col_group * WAYS + r)

        loop(WAYS, one)

    factor = 1.0 / math.sqrt(TOK * N)

    def finish_up(kind):
        arrived(kind, acc_u)
        total = acc_u[0]
        for i in range(1, WAYS):
            total = total + acc_u[i]
        total = total * factor
        for r in range(WAYS):
            slab[r, 0:4, :] = total[4 * r : 4 * r + 4, :]
        loop(WAYS, lambda r: push_or_keep(slab.at[r], slab_in.at[col_group], UPB, row_group * WAYS + r))

    def finish():
        arrived(UPB, slab_in)
        for j in range(WAYS):
            ugrad_ref[0, :, COLS * j : COLS * (j + 1)] = slab_in[j, 0:4, :]
        arrived(DOWN, acc_d)
        total = acc_d[0]
        for i in range(1, WAYS):
            total = total + acc_d[i]
        dgrad_ref[0] = total * factor
        left(UPB, slab.at[pl.ds(0, WAYS - 1)])

        @pl.when(row_group == col_group)
        def _():
            left(DOWN, acc_d.at[pl.ds(0, WAYS - 1)])

        @pl.when(row_group != col_group)
        def _():
            left(DOWN, acc_d)

    @pl.when(first)
    def _():
        squares = lax.fori_loop(
            0, WAYS,
            lambda t, c: c + jnp.sum(jnp.square(own_ref[0, :, tile(t)].astype(F32)), axis=1, keepdims=True),
            jnp.zeros((TOK, 1), F32),
        )
        inverse = lax.rsqrt(squares * (1.0 / WIDTH) + 1e-06)
        inv_ref[0:TOK, :] = jnp.broadcast_to(inverse, (TOK, 128))
        act_ref[0:TOK, :] = jnp.zeros((TOK, RANK), F32)

        def enter(t):
            cols = tile(t)
            v = own_ref[0, :, cols].astype(F32)
            n = (v * inverse * gain_ref[0, :, cols].astype(F32)).astype(BF)
            normed[:, cols] = n
            act_ref[0:TOK, :] += nn(n, down_ref[0, 0, cols, :])

        loop(WAYS, enter)
        act = act_ref[0:TOK, :]
        sq_out[...] = (act * jax.nn.sigmoid(act)).astype(BF)
        all_here()

        def leave(t):
            j = lax.rem(t + p, WAYS)
            cols = tile(j)
            v = own_ref[0, :, cols].astype(F32)
            hid[:, cols] = (v + nn(sq_out[...], up_ref[0, 0, :, cols])).astype(BF)
            loop(WAYS, lambda i: push(hid.at[strip(i), cols], pieces.at[p], ENDS, 1, i * WAYS + j))

        loop(WAYS, leave)
        arrived(ENDS, pieces)
        choose_and_send(COT, cot_in)

        def extras(k):
            t = target(p, k)
            i, j = t // WAYS, lax.rem(t, WAYS)
            push_or_keep(normed.at[strip(i), tile(j)], norm_in.at[p], NORM, t)
            push_or_keep(sq_out.at[strip(i)], sq0_in.at[p], SQ0, t)

        loop(N, extras)

        arrived(BACK, back_in)

        def home(k):
            t = target(p, k)
            bnd_pick[t] = back_in[back_ref[0, t]]
            push_or_keep(bnd_pick.at[t], bnd.at[my_rows, my_cols], BND0, t)

        loop(N, home)

        def home1(k):
            t = target(p, k)
            push(bnd_pick.at[t], ends_ref.at[0, my_rows, my_cols], BND1, 1, t)

        loop(N, home1)
        arrived(SQ1, sq1_in)

        def choose_sq(t):
            sq_pick[t] = sq1_in[back_ref[0, t]]

        loop(N, choose_sq)
        arrived(SQ0, sq0_in)
        partial(part_u, sq0_in, bnd_pick)
        send_up(part_u, UPA, 0)
        partial(part_u1, sq_pick, pieces)
        send_up(part_u1, UPA1, 1)

        arrived(BND0, bnd)
        gsq_ref[0:TOK, :] = jnp.zeros((TOK, RANK), F32)

        def into(t):
            cols = tile(t)
            gsq_ref[0:TOK, :] += nt(bnd[:, cols], up_ref[0, 0, :, cols])

        loop(WAYS, into)
        act2 = act_ref[0:TOK, :]
        _, ga = middle(act2, gsq_ref[0:TOK, :])
        ga_out[...] = ga
        loop(N, lambda k: push_or_keep(ga_out.at[strip(target(p, k) // WAYS)], ga0_in.at[p], GA0, target(p, k)))
        inv2 = inv_ref[0:TOK, 0:1]
        dots = jnp.sum(ga.astype(F32) * act2, axis=1, keepdims=True) * (1.0 / WIDTH)
        pull = inv2 * inv2 * dots

        def out(t):
            cols = tile(t)
            gn = nt(ga_out[...], down_ref[0, 0, cols, :]) * gain_ref[0, :, cols].astype(F32)
            v = own_ref[0, :, cols].astype(F32)
            ends_ref[0, :, cols] = (bnd[:, cols].astype(F32) + inv2 * gn - v * pull).astype(BF)

        loop(WAYS, out)
        finish_up(UPA)
        arrived(NORM, norm_in)
        arrived(GA0, ga0_in)
        partial(part_d, norm_in, ga0_in)
        send_down()
        finish()
        left(ENDS, pieces)
        left(COT, cot_in)
        left(NORM, norm_in.at[pl.ds(0, N - 1)])
        left(SQ0, sq0_in.at[pl.ds(0, N - 1)])
        left(BND0, bnd_pick.at[pl.ds(0, N - 1)])
        left(BND1, bnd_pick)
        left(GA0, ga0_in.at[pl.ds(0, N - 1)])
        left(UPA, acc_u.at[pl.ds(0, WAYS - 1)])
        left(UPA1, acc_u)

    @pl.when(second)
    def _():
        for j in range(WAYS):
            for c in range(COLS // 128):
                at = COLS * j + 128 * c
                gain_out[j, c : c + 1, :] = gain_ref[0, :, at : at + 128].astype(F32)
        all_here()

        def spread(k):
            t = target(p, k)
            push(own_ref.at[0, strip(t // WAYS), tile(lax.rem(t, WAYS))], pieces.at[p], ENDS, 0, t)

        loop(N, spread)

        def gains(k):
            t = target(p, k)
            push_or_keep(gain_out.at[lax.rem(t, WAYS)], gain_in.at[p], GAIN, t)

        loop(N, gains)
        arrived(ENDS, pieces)
        choose_and_send(HID, hid_in)
        arrived(HID, hid_in)

        rows = 2 * TOK
        squares = lax.fori_loop(
            0, WAYS,
            lambda t, c: c + jnp.sum(jnp.square(hid_in[:, :, tile(t)].reshape(rows, COLS).astype(F32)), axis=1, keepdims=True),
            jnp.zeros((rows, 1), F32),
        )
        inverse = lax.rsqrt(squares * (1.0 / WIDTH) + 1e-06)
        act_ref[...] = jnp.zeros((rows, RANK), F32)

        def enter(t):
            cols = tile(t)
            v = hid_in[:, :, cols].reshape(rows, COLS).astype(F32)
            n = (v * inverse * gain_ref[0, :, cols].astype(F32)).astype(BF)
            act_ref[...] += nn(n, down_ref[0, 0, cols, :])

        loop(WAYS, enter)
        arrived(COT, cot_in)
        gsq_ref[...] = jnp.zeros((rows, RANK), F32)

        def into(t):
            cols = tile(t)
            gsq_ref[...] += nt(cot_in[:, :, cols].reshape(rows, COLS), up_ref[0, 0, :, cols])

        loop(WAYS, into)
        act = act_ref[...]
        squashed, ga = middle(act, gsq_ref[...])
        sq_slots[...] = squashed.reshape(2, TOK, RANK)
        ga32 = ga.astype(F32)
        ga_slots[...] = (ga32 * inverse).astype(BF).reshape(2, TOK, RANK)
        dots = jnp.sum(ga32 * act, axis=1, keepdims=True) * (1.0 / WIDTH)
        pull = inverse * inverse * dots

        def out(t):
            j = lax.rem(t + p, WAYS)
            cols = tile(j)
            gn = nt(ga, down_ref[0, 0, cols, :]) * gain_ref[0, :, cols].astype(F32)
            v = hid_in[:, :, cols].reshape(rows, COLS).astype(F32)
            c = cot_in[:, :, cols].reshape(rows, COLS).astype(F32)
            cot_in[:, :, cols] = (c + inverse * gn - v * pull).astype(BF).reshape(2, TOK, COLS)
            loop(
                WAYS,
                lambda i: push(cot_in.at[:, strip(i), cols], back_in.at[pl.ds(2 * p, 2)], BACK, 0, i * WAYS + j),
            )

        loop(WAYS, out)

        def extras(k):
            t = target(p, k)
            at = strip(t // WAYS)
            push(sq_slots.at[:, at], sq1_in.at[pl.ds(2 * p, 2)], SQ1, 0, t)
            push_or_keep(ga_slots.at[:, at], ga1_in.at[pl.ds(2 * p, 2)], GA1, t)

        loop(N, extras)
        arrived(GAIN, gain_in)
        arrived(GA1, ga1_in)

        def choose_ga(t):
            at = back_ref[0, t]
            sq_pick[t] = ga1_in[at]
            g = gain_in[lax.div(at, 2)]
            for c in range(COLS // 128):
                cols = pl.ds(128 * c, 128)
                norm_in[t, :, cols] = (pieces[t, :, cols].astype(F32) * g[c : c + 1, :]).astype(BF)

        loop(N, choose_ga)
        partial(part_d, norm_in, sq_pick)
        send_down()
        finish_up(UPA1)
        finish()
        arrived(BND1, ends_ref.at[0])
        left(ENDS, pieces)
        left(GAIN, gain_in.at[pl.ds(0, N - 1)])
        left(HID, picked.at[pl.ds(0, N - 1)])
        left(BACK, back_in)
        left(SQ1, sq1_in)
        left(GA1, ga1_in.at[pl.ds(0, 2 * N - 2)])


def shards(batch_ends, wiring, down_proj, up_proj, norm_gain):
    ids = jnp.arange(N, dtype=jnp.int32)
    goes = wiring[:, None] == ids[None, :]
    earliest = jnp.min(jnp.where(goes, ids[:, None], N), axis=0)
    latest = jnp.max(jnp.where(goes, ids[:, None], -1), axis=0)
    sources = jnp.stack([jnp.where(earliest == N, 0, earliest), jnp.maximum(latest, 0)])
    again = jnp.any((wiring[:, None] == wiring[None, :]) & (ids[None, :] < ids[:, None]), axis=1)
    slots = (2 * wiring + again.astype(jnp.int32))[None]
    vmem = pl.BlockSpec(memory_space=pltpu.VMEM)
    smem = pl.BlockSpec(memory_space=pltpu.SMEM)
    block = (TOK, WIDTH)
    scratch = [
        pltpu.VMEM((N, ROWS, COLS), BF),
        pltpu.VMEM((N, 2, ROWS, COLS), BF),
        pltpu.VMEM(block, BF),
        pltpu.VMEM(block, BF),
        pltpu.VMEM((2, *block), BF),
        pltpu.VMEM((2, *block), BF),
        pltpu.VMEM((WAYS, 8, 128), F32),
        pltpu.VMEM((N, 8, 128), F32),
        pltpu.VMEM((N, ROWS, COLS), BF),
        pltpu.VMEM((TOK, RANK), BF),
        pltpu.VMEM((N, ROWS, RANK), BF),
        pltpu.VMEM((2, TOK, RANK), BF),
        pltpu.VMEM((2, TOK, RANK), BF),
        pltpu.VMEM((2 * N, ROWS, COLS), BF),
        pltpu.VMEM((2 * N, ROWS, RANK), BF),
        pltpu.VMEM((2 * N, ROWS, RANK), BF),
        pltpu.VMEM((N, ROWS, COLS), BF),
        pltpu.VMEM(block, BF),
        pltpu.VMEM((N, ROWS, RANK), BF),
        pltpu.VMEM((TOK, RANK), BF),
        pltpu.VMEM((N, ROWS, RANK), BF),
        pltpu.VMEM((2 * TOK, RANK), F32),
        pltpu.VMEM((2 * TOK, RANK), F32),
        pltpu.VMEM((TOK, 128), F32),
        pltpu.VMEM((COLS, RANK), F32),
        pltpu.VMEM((RANK, COLS), F32),
        pltpu.VMEM((RANK, COLS), F32),
        pltpu.VMEM((WAYS, 80, RANK), F32),
        pltpu.VMEM((WAYS, 32, COLS), F32),
        pltpu.VMEM((WAYS, 8, COLS), F32),
        pltpu.VMEM((WAYS, 8, COLS), F32),
        pltpu.SemaphoreType.DMA((CLASSES,)),
        pltpu.SemaphoreType.DMA((CLASSES,)),
    ]
    return pl.pallas_call(
        step_kernel,
        out_shape=(
            jax.ShapeDtypeStruct((1, *block), BF),
            jax.ShapeDtypeStruct((1, WIDTH // N, RANK), F32),
            jax.ShapeDtypeStruct((1, RANK // N, WIDTH), F32),
        ),
        in_specs=[smem, smem, vmem, vmem, vmem, vmem],
        out_specs=(vmem, vmem, vmem),
        scratch_shapes=scratch,
        compiler_params=pltpu.CompilerParams(
            collective_id=0, has_side_effects=True, vmem_limit_bytes=56 * 1024 * 1024
        ),
        name="adapter_step",
    )(sources, slots, batch_ends, down_proj, up_proj, norm_gain)


def solution(mesh):
    return jax.shard_map(
        shards,
        mesh=mesh,
        in_specs=(
            P("section", "peer", None),
            P(),
            P("section", "peer", None, None),
            P("section", "peer", None, None),
            P("section", "peer", None),
        ),
        out_specs=(
            P("section", "peer", None),
            P("section", "peer", None),
            P("section", "peer", None),
        ),
        check_vma=False,
    )
```

```python
import functools
import math

import jax
import jax.numpy as jnp
from jax import lax
from jax.experimental import pallas as pl
from jax.experimental.pallas import tpu as pltpu
from jax.sharding import PartitionSpec as P

N = 64
ROWS = 16
COLS = 640
WAYS = 8
TOK, WIDTH, RANK = 128, 5120, 256
BF, F32 = jnp.bfloat16, jnp.float32
MESH = pl.DeviceIdType.MESH

STAGES = 2
GROUPS = WAYS // STAGES
PART = TOK // STAGES
WIDE = 1280

(ENDS, GAIN, NORM, SQ0, BACK, SQ1, GA1, BND1, GA0, DOWN, DOWN0, UPA, UPA1, UPB) = range(14)
COT, HID, BND0 = 14, 14 + STAGES, 14 + 2 * STAGES
CLASSES = 14 + 3 * STAGES
(OWN, DOWN_W, UP_W, TABLE, LOADS) = range(5)


def target(p, k):
    a = lax.rem(lax.rem(k, 4) + 2 * lax.rem(p, 2), 4)
    b = lax.rem(k // 4, 4)
    x = lax.rem(p // 16 + a, 4)
    y = lax.rem(lax.rem(p // 4, 4) + a + b, 4)
    z = lax.rem(lax.rem(p // 2, 2) + lax.rem(k // 16, 2) + a, 2)
    core = lax.rem(lax.rem(p, 2) + k // 32 + a // 2, 2)
    return x * 16 + y * 4 + z * 2 + core


def place(k):
    m = k // 2
    return lax.rem(k, 2) * GROUPS + m // WAYS, lax.rem(m, WAYS)


def holder(i, j):
    return 2 * (lax.rem(i, GROUPS) * WAYS + j) + i // GROUPS


def mate(p, stage, m):
    a = lax.rem(lax.rem(m, 4) + 2 * lax.rem(p, 2), 4)
    b = lax.rem(m // 4, 4)
    x = lax.rem(p // 16 + a, 4)
    y = lax.rem(lax.rem(p // 4, 4) + a + b, 4)
    z = lax.rem(lax.rem(p // 2, 2) + m // 16 + a, 2)
    return x * 16 + y * 4 + z * 2 + stage


def nn(left, right):
    return jnp.dot(left, right, preferred_element_type=F32)


def nt(left, right):
    return lax.dot_general(left, right, (((1,), (1,)), ((), ())), preferred_element_type=F32)


def tn(left, right):
    return lax.dot_general(left, right, (((0,), (0,)), ((), ())), preferred_element_type=F32)


def loop(count, body):
    def step(k, carry):
        body(k)
        return carry

    lax.fori_loop(0, count, step, 0)


def tile(t):
    return pl.ds(pl.multiple_of(t * COLS, 128), COLS)


def wide(t):
    return pl.ds(pl.multiple_of(t * WIDE, 128), WIDE)


def strip(i):
    return pl.ds(pl.multiple_of(i * ROWS, ROWS), ROWS)


def step_kernel(
    wiring_ref, gain_ref, own_any, down_any, up_any,
    ends_ref, dgrad_ref, ugrad_ref,
    own, down, up, pieces, picked, hid, normed, hid_in, cot_in, gain_out, gain_in, norm_in,
    sq_out, sq0_in, sq_slots, ga_slots, back_in, sq1_in, ga1_in, gathered, bnd, sq_pick,
    ga_out, ga0_in, act_ref, gsq_ref, inv_ref, part_d, part_u, small_d, small_d0, small_u, small_u1,
    acc_d, acc_u, slab, slab_in, table_v, table,
    load, send, recv,
):
    s = lax.axis_index("section")
    p = lax.axis_index("peer")
    first, second = s == 0, s == 1
    my_i, my_j = place(p)
    my_stage = my_i // GROUPS
    my_rows, my_cols = strip(my_i), tile(my_j)

    def push(src, dst, kind, section, peer, out=None):
        pltpu.make_async_remote_copy(
            src_ref=src, dst_ref=dst, send_sem=send.at[kind if out is None else out], recv_sem=recv.at[kind],
            device_id={"section": section, "peer": peer}, device_id_type=MESH,
        ).start()

    def push_or_keep(src, dst, kind, peer, out=None):
        @pl.when(peer != p)
        def _():
            push(src, dst, kind, s, peer, out)

        @pl.when(peer == p)
        def _():
            pltpu.make_async_copy(src, dst, recv.at[kind]).start()

    def arrived(kind, ref):
        pltpu.make_async_copy(ref, ref, recv.at[kind]).wait()

    def left(kind, ref):
        pltpu.make_async_copy(ref, ref, send.at[kind]).wait()

    own_load = pltpu.make_async_copy(own_any.at[0], own, load.at[OWN])
    down_load = pltpu.make_async_copy(down_any.at[0, 0], down, load.at[DOWN_W])
    up_load = pltpu.make_async_copy(up_any.at[0, 0], up, load.at[UP_W])
    table_load = pltpu.make_async_copy(table_v, table, load.at[TABLE])
    own_load.start()
    down_load.start()
    up_load.start()

    barrier = pltpu.get_barrier_semaphore()

    def greet(k):
        t = target(p, k)
        pl.semaphore_signal(barrier, inc=1, device_id={"section": 1 - s, "peer": t}, device_id_type=MESH)

        @pl.when(t != p)
        def _():
            pl.semaphore_signal(barrier, inc=1, device_id={"section": s, "peer": t}, device_id_type=MESH)

    loop(N, greet)

    def all_here():
        pl.semaphore_wait(barrier, 2 * N - 1)

    def make_table():
        lane = lax.broadcasted_iota(jnp.int32, (N, N), 1)
        line = lax.broadcasted_iota(jnp.int32, (N, N), 0)
        wired = jnp.broadcast_to(wiring_ref[...], (N, N))
        goes = wired == line
        earliest = jnp.min(jnp.where(goes, lane, N), axis=1, keepdims=True)
        latest = jnp.max(jnp.where(goes, lane, -1), axis=1, keepdims=True)
        mine = jnp.max(jnp.where(lane == line, wired, 0), axis=1, keepdims=True)
        again = jnp.max(jnp.where((wired == mine) & (lane < line), 1, 0), axis=1, keepdims=True)
        column = lax.broadcasted_iota(jnp.int32, (N, 128), 1)
        table_v[...] = jnp.where(
            column == 0,
            jnp.where(earliest == N, 0, earliest),
            jnp.where(column == 1, jnp.maximum(latest, 0), 2 * mine + again),
        )
        table_load.start()

    def choose_and_send(kind, dst_ref):
        def one(k):
            q = target(p, k)
            picked[q, 0] = pieces[table[q, 0]]
            picked[q, 1] = pieces[table[q, 1]]
            dst = dst_ref.at[:, my_rows, my_cols]
            if kind == HID:
                push_or_keep(picked.at[q], dst, kind + my_stage, q, kind)
            else:
                push(picked.at[q], dst, kind + my_stage, 1, q, kind)

        loop(N, one)

    def middle(act, gsq):
        sig = jax.nn.sigmoid(act)
        squashed = (act * sig).astype(BF)
        ga = (gsq * sig * (1.0 + act * (1.0 - sig))).astype(BF)
        return squashed, ga

    def partial(small, out, left_ref, right_ref):
        out[...] = jnp.zeros_like(out)

        def some(t):
            rows = pl.ds(t * 16, 16)
            a = left_ref[rows].reshape(16 * ROWS, left_ref.shape[2])
            b = right_ref[rows].reshape(16 * ROWS, right_ref.shape[2])
            out[...] += tn(a, b)

        loop(4, some)
        small[...] = out[...].astype(BF)

    def send_up(part, kind):
        def one(i):
            src = part.at[pl.ds(pl.multiple_of(i * 32, 32), 32)]
            dst = acc_u.at[my_i]
            peer = holder(i, my_j)
            if kind == UPA:
                push_or_keep(src, dst, kind, peer)
            else:
                push(src, dst, kind, 1, peer)

        loop(WAYS, one)

    def send_down(part, kind):
        def one(r):
            src = part.at[pl.ds(pl.multiple_of(r * 80, 16), 80)]
            peer = my_j * WAYS + r
            if kind == DOWN:
                push_or_keep(src, acc_d.at[my_i], kind, peer)
            else:
                push(src, acc_d.at[my_i], kind, 0, peer)

        loop(WAYS, one)

    factor = 1.0 / math.sqrt(TOK * N)

    def total_of(acc):
        total = acc[0].astype(F32)
        for i in range(1, WAYS):
            total = total + acc[i].astype(F32)
        return total * factor

    def finish_up(kind):
        arrived(kind, acc_u)
        total = total_of(acc_u)
        for r in range(WAYS):
            slab[r, 0:4, :] = total[4 * r : 4 * r + 4, :]
        loop(WAYS, lambda r: push_or_keep(slab.at[r], slab_in.at[my_j], UPB, my_i * WAYS + r))

    def left_but_own(kind, ref, has_own):
        @pl.when(has_own)
        def _():
            left(kind, ref.at[pl.ds(0, WAYS - 1)])

        @pl.when(jnp.logical_not(has_own))
        def _():
            left(kind, ref)

    def finish(kind):
        arrived(UPB, slab_in)
        for j in range(WAYS):
            ugrad_ref[0, :, COLS * j : COLS * (j + 1)] = slab_in[j, 0:4, :]
        arrived(kind, acc_d)
        dgrad_ref[0] = total_of(acc_d)
        left_but_own(UPB, slab, my_i == p // WAYS)

    @pl.when(first)
    def _():
        own_load.wait()

        def forward(stage):
            rows = pl.ds(pl.multiple_of(stage * PART, PART), PART)
            squares = lax.fori_loop(
                0, WIDTH // WIDE,
                lambda t, c: c + jnp.sum(jnp.square(own[rows, wide(t)].astype(F32)), axis=1, keepdims=True),
                jnp.zeros((PART, 1), F32),
            )
            inverse = lax.rsqrt(squares * (1.0 / WIDTH) + 1e-06)
            inv_ref[rows, :] = jnp.broadcast_to(inverse, (PART, 128))
            act_ref[rows, :] = jnp.zeros((PART, RANK), F32)

            @pl.when(stage == 0)
            def _():
                down_load.wait()

            def enter(t):
                cols = wide(t)
                v = own[rows, cols].astype(F32)
                n = (v * inverse * gain_ref[0, :, cols].astype(F32)).astype(BF)
                normed[rows, cols] = n
                act_ref[rows, :] += nn(n, down[cols, :])

            loop(WIDTH // WIDE, enter)
            act = act_ref[rows, :]
            sq_out[rows, :] = (act * jax.nn.sigmoid(act)).astype(BF)

            @pl.when(stage == 0)
            def _():
                up_load.wait()

            def leave(t):
                cols = wide(t)
                v = own[rows, cols].astype(F32)
                hid[rows, cols] = (v + nn(sq_out[rows, :], up[:, cols])).astype(BF)

            loop(WIDTH // WIDE, leave)

            @pl.when(stage == 0)
            def _():
                all_here()

            def spread(m):
                t = mate(p, stage, m)
                i, j = place(t)
                push(hid.at[strip(i), tile(j)], pieces.at[p], ENDS, 1, t)

            loop(N // STAGES, spread)

        loop(STAGES, forward)
        make_table()
        table_load.wait()
        arrived(ENDS, pieces)
        choose_and_send(COT, cot_in)

        def backward(stage):
            rows = pl.ds(pl.multiple_of(stage * PART, PART), PART)

            @pl.when(stage == my_stage)
            def _():
                arrived(BACK, back_in)

                def home(k):
                    t = target(p, k)
                    gathered[t] = back_in[table[t, 2]]
                    push_or_keep(gathered.at[t], bnd.at[my_rows, my_cols], BND0 + stage, t, BND0)

                loop(N, home)

                def home1(k):
                    t = target(p, k)
                    push(gathered.at[t], ends_ref.at[0, my_rows, my_cols], BND1, 1, t)

                loop(N, home1)

            arrived(BND0 + stage, bnd.at[rows, :])
            gsq_ref[rows, :] = jnp.zeros((PART, RANK), F32)

            def into(t):
                cols = wide(t)
                gsq_ref[rows, :] += nt(bnd[rows, cols], up[:, cols])

            loop(WIDTH // WIDE, into)
            act = act_ref[rows, :]
            _, ga = middle(act, gsq_ref[rows, :])
            ga_out[rows, :] = ga

            def give(m):
                t = mate(p, stage, m)
                i, _ = place(t)
                push(ga_out.at[strip(i)], ga0_in.at[p], GA0, 1, t)

            loop(N // STAGES, give)
            inverse = inv_ref[rows, 0:1]
            dots = jnp.sum(ga.astype(F32) * act, axis=1, keepdims=True) * (1.0 / WIDTH)
            pull = inverse * inverse * dots

            def out(t):
                cols = wide(t)
                gn = nt(ga_out[rows, :], down[cols, :]) * gain_ref[0, :, cols].astype(F32)
                v = own[rows, cols].astype(F32)
                ends_ref[0, rows, cols] = (bnd[rows, cols].astype(F32) + inverse * gn - v * pull).astype(BF)

            loop(WIDTH // WIDE, out)

            @pl.when(stage == 0)
            def _():
                def extras(k):
                    t = target(p, k)
                    i, j = place(t)
                    push(normed.at[strip(i), tile(j)], norm_in.at[p], NORM, 1, t)
                    push_or_keep(sq_out.at[strip(i)], sq0_in.at[p], SQ0, t)

                loop(N, extras)

        loop(STAGES, backward)
        arrived(SQ0, sq0_in)
        partial(small_u, part_u, sq0_in, gathered)
        send_up(small_u, UPA)
        arrived(SQ1, sq1_in)

        def choose_sq(t):
            sq_pick[t] = sq1_in[table[t, 2]]

        loop(N, choose_sq)
        partial(small_u1, part_u, sq_pick, pieces)
        send_up(small_u1, UPA1)
        finish_up(UPA)
        finish(DOWN0)
        left(ENDS, pieces)
        left(COT, cot_in)
        left(NORM, norm_in)
        left(SQ0, sq0_in.at[pl.ds(0, N - 1)])
        left(BND0, gathered.at[pl.ds(0, N - 1)])
        left(BND1, gathered)
        left(GA0, ga0_in)
        left(UPA, acc_u.at[pl.ds(0, WAYS - 1)])
        left(UPA1, acc_u)

    @pl.when(second)
    def _():
        own_load.wait()
        all_here()

        def spread(stage):
            def one(m):
                t = mate(p, stage, m)
                i, j = place(t)
                push(own.at[strip(i), tile(j)], pieces.at[p], ENDS, 0, t)

            loop(N // STAGES, one)

        loop(STAGES, spread)
        make_table()
        for j in range(WAYS):
            for c in range(COLS // 128):
                at = COLS * j + 128 * c
                gain_out[j, c : c + 1, :] = gain_ref[0, :, at : at + 128].astype(F32)
        table_load.wait()
        down_load.wait()
        up_load.wait()
        arrived(ENDS, pieces)
        choose_and_send(HID, hid_in)
        both = 2 * PART

        def through(stage):
            rows = pl.ds(pl.multiple_of(stage * PART, PART), PART)
            arrived(HID + stage, hid_in.at[:, rows, :])
            squares = lax.fori_loop(
                0, WIDTH // WIDE,
                lambda t, c: c
                + jnp.sum(jnp.square(hid_in[:, rows, wide(t)].reshape(both, WIDE).astype(F32)), axis=1, keepdims=True),
                jnp.zeros((both, 1), F32),
            )
            inverse = lax.rsqrt(squares * (1.0 / WIDTH) + 1e-06)
            act_ref[0:both, :] = jnp.zeros((both, RANK), F32)

            def enter(t):
                cols = wide(t)
                v = hid_in[:, rows, cols].reshape(both, WIDE).astype(F32)
                n = (v * inverse * gain_ref[0, :, cols].astype(F32)).astype(BF)
                act_ref[0:both, :] += nn(n, down[cols, :])

            loop(WIDTH // WIDE, enter)
            arrived(COT + stage, cot_in.at[:, rows, :])
            gsq_ref[0:both, :] = jnp.zeros((both, RANK), F32)

            def into(t):
                cols = wide(t)
                gsq_ref[0:both, :] += nt(cot_in[:, rows, cols].reshape(both, WIDE), up[:, cols])

            loop(WIDTH // WIDE, into)
            act = act_ref[0:both, :]
            squashed, ga = middle(act, gsq_ref[0:both, :])
            sq_slots[:, rows, :] = squashed.reshape(2, PART, RANK)
            ga32 = ga.astype(F32)
            ga_slots[:, rows, :] = (ga32 * inverse).astype(BF).reshape(2, PART, RANK)
            dots = jnp.sum(ga32 * act, axis=1, keepdims=True) * (1.0 / WIDTH)
            pull = inverse * inverse * dots

            def out(t):
                u = lax.rem(t + p, WIDTH // WIDE)
                cols = wide(u)
                gn = nt(ga, down[cols, :]) * gain_ref[0, :, cols].astype(F32)
                v = hid_in[:, rows, cols].reshape(both, WIDE).astype(F32)
                c = cot_in[:, rows, cols].reshape(both, WIDE).astype(F32)
                cot_in[:, rows, cols] = (c + inverse * gn - v * pull).astype(BF).reshape(2, PART, WIDE)

                def give(n):
                    i = stage * GROUPS + lax.rem(n, GROUPS)
                    j = u * (WIDE // COLS) + n // GROUPS
                    push(cot_in.at[:, strip(i), tile(j)], back_in.at[pl.ds(2 * p, 2)], BACK, 0, holder(i, j))

                loop(GROUPS * WIDE // COLS, give)

            loop(WIDTH // WIDE, out)

        loop(STAGES, through)

        def extras(k):
            t = target(p, k)
            i, j = place(t)
            push(sq_slots.at[:, strip(i)], sq1_in.at[pl.ds(2 * p, 2)], SQ1, 0, t)
            push_or_keep(ga_slots.at[:, strip(i)], ga1_in.at[pl.ds(2 * p, 2)], GA1, t)
            push_or_keep(gain_out.at[j], gain_in.at[p], GAIN, t)

        loop(N, extras)
        arrived(GAIN, gain_in)
        arrived(GA1, ga1_in)

        def choose_ga(t):
            at = table[t, 2]
            sq_pick[t] = ga1_in[at]
            g = gain_in[lax.div(at, 2)]
            for c in range(COLS // 128):
                cols = pl.ds(128 * c, 128)
                gathered[t, :, cols] = (pieces[t, :, cols].astype(F32) * g[c : c + 1, :]).astype(BF)

        loop(N, choose_ga)
        partial(small_d, part_d, gathered, sq_pick)
        send_down(small_d, DOWN)
        arrived(NORM, norm_in)
        arrived(GA0, ga0_in)
        partial(small_d0, part_d, norm_in, ga0_in)
        send_down(small_d0, DOWN0)
        finish_up(UPA1)
        finish(DOWN)
        arrived(BND1, ends_ref.at[0])
        left(ENDS, pieces)
        left(GAIN, gain_in.at[pl.ds(0, N - 1)])
        left(HID, picked.at[pl.ds(0, N - 1)])
        left(BACK, back_in)
        left(SQ1, sq1_in)
        left(GA1, ga1_in.at[pl.ds(0, 2 * N - 2)])
        left_but_own(DOWN, acc_d, my_j == p // WAYS)
        left(DOWN0, acc_d)


def shards(batch_ends, wiring, down_proj, up_proj, norm_gain):
    vmem = pl.BlockSpec(memory_space=pltpu.VMEM)
    hbm = pl.BlockSpec(memory_space=pl.ANY)
    block = (TOK, WIDTH)
    scratch = [
        pltpu.VMEM(block, BF),
        pltpu.VMEM((WIDTH, RANK), BF),
        pltpu.VMEM((RANK, WIDTH), BF),
        pltpu.VMEM((N, ROWS, COLS), BF),
        pltpu.VMEM((N, 2, ROWS, COLS), BF),
        pltpu.VMEM(block, BF),
        pltpu.VMEM(block, BF),
        pltpu.VMEM((2, *block), BF),
        pltpu.VMEM((2, *block), BF),
        pltpu.VMEM((WAYS, 8, 128), F32),
        pltpu.VMEM((N, 8, 128), F32),
        pltpu.VMEM((N, ROWS, COLS), BF),
        pltpu.VMEM((TOK, RANK), BF),
        pltpu.VMEM((N, ROWS, RANK), BF),
        pltpu.VMEM((2, TOK, RANK), BF),
        pltpu.VMEM((2, TOK, RANK), BF),
        pltpu.VMEM((2 * N, ROWS, COLS), BF),
        pltpu.VMEM((2 * N, ROWS, RANK), BF),
        pltpu.VMEM((2 * N, ROWS, RANK), BF),
        pltpu.VMEM((N, ROWS, COLS), BF),
        pltpu.VMEM(block, BF),
        pltpu.VMEM((N, ROWS, RANK), BF),
        pltpu.VMEM((TOK, RANK), BF),
        pltpu.VMEM((N, ROWS, RANK), BF),
        pltpu.VMEM((2 * TOK, RANK), F32),
        pltpu.VMEM((2 * TOK, RANK), F32),
        pltpu.VMEM((TOK, 128), F32),
        pltpu.VMEM((COLS, RANK), F32),
        pltpu.VMEM((RANK, COLS), F32),
        pltpu.VMEM((COLS, RANK), BF),
        pltpu.VMEM((COLS, RANK), BF),
        pltpu.VMEM((RANK, COLS), BF),
        pltpu.VMEM((RANK, COLS), BF),
        pltpu.VMEM((WAYS, 80, RANK), BF),
        pltpu.VMEM((WAYS, 32, COLS), BF),
        pltpu.VMEM((WAYS, 8, COLS), F32),
        pltpu.VMEM((WAYS, 8, COLS), F32),
        pltpu.VMEM((N, 128), jnp.int32),
        pltpu.SMEM((N, 128), jnp.int32),
        pltpu.SemaphoreType.DMA((LOADS,)),
        pltpu.SemaphoreType.DMA((CLASSES,)),
        pltpu.SemaphoreType.DMA((CLASSES,)),
    ]
    return pl.pallas_call(
        step_kernel,
        out_shape=(
            jax.ShapeDtypeStruct((1, *block), BF),
            jax.ShapeDtypeStruct((1, WIDTH // N, RANK), F32),
            jax.ShapeDtypeStruct((1, RANK // N, WIDTH), F32),
        ),
        in_specs=[vmem, vmem, hbm, hbm, hbm],
        out_specs=(vmem, vmem, vmem),
        scratch_shapes=scratch,
        compiler_params=pltpu.CompilerParams(
            collective_id=0, has_side_effects=True, vmem_limit_bytes=56 * 1024 * 1024
        ),
        name="adapter_step",
    )(wiring[None], norm_gain, batch_ends, down_proj, up_proj)


def solution(mesh):
    return jax.shard_map(
        shards,
        mesh=mesh,
        in_specs=(
            P("section", "peer", None),
            P(),
            P("section", "peer", None, None),
            P("section", "peer", None, None),
            P("section", "peer", None),
        ),
        out_specs=(
            P("section", "peer", None),
            P("section", "peer", None),
            P("section", "peer", None),
        ),
        check_vma=False,
    )
```

```python
import functools
import math

import jax
import jax.numpy as jnp
from jax import lax
from jax.experimental import pallas as pl
from jax.experimental.pallas import tpu as pltpu
from jax.sharding import PartitionSpec as P

N = 64
ROWS = 16
COLS = 640
WAYS = 8
TOK, WIDTH, RANK = 128, 5120, 256
BF, F32 = jnp.bfloat16, jnp.float32
MESH = pl.DeviceIdType.MESH

STAGES = 2
GROUPS = WAYS // STAGES
PART = TOK // STAGES
WIDE = 1280

(ENDS, ENDH, GAIN, NORM, SQ0, COT, COT_LATE, HID, BOTH, BACK, SG, SQF, GAF, BND1, GA0, DOWN, DOWN1, UPA, UPA1, UPB, BND0) = range(21)
CLASSES = 20 + STAGES
EARLY = 16
CHUNK = 128
(OWN, DOWN_W, UP_W, TABLE, LOADS) = range(5)


def target(p, k):
    a = lax.rem(lax.rem(k, 4) + 2 * lax.rem(p, 2), 4)
    b = lax.rem(k // 4, 4)
    x = lax.rem(p // 16 + a, 4)
    y = lax.rem(lax.rem(p // 4, 4) + a + b, 4)
    z = lax.rem(lax.rem(p // 2, 2) + lax.rem(k // 16, 2) + a, 2)
    core = lax.rem(lax.rem(p, 2) + k // 32 + a // 2, 2)
    return x * 16 + y * 4 + z * 2 + core


def place(k):
    m = k // 2
    return lax.rem(k, 2) * GROUPS + m // WAYS, lax.rem(m, WAYS)


def holder(i, j):
    return 2 * (lax.rem(i, GROUPS) * WAYS + j) + i // GROUPS


def mate(p, stage, m):
    a = lax.rem(lax.rem(m, 4) + 2 * lax.rem(p, 2), 4)
    b = lax.rem(m // 4, 4)
    x = lax.rem(p // 16 + a, 4)
    y = lax.rem(lax.rem(p // 4, 4) + a + b, 4)
    z = lax.rem(lax.rem(p // 2, 2) + m // 16 + a, 2)
    return x * 16 + y * 4 + z * 2 + stage


def nn(left, right):
    return jnp.dot(left, right, preferred_element_type=F32)


def nt(left, right):
    return lax.dot_general(left, right, (((1,), (1,)), ((), ())), preferred_element_type=F32)


def tn(left, right):
    return lax.dot_general(left, right, (((0,), (0,)), ((), ())), preferred_element_type=F32)


def loop(count, body):
    def step(k, carry):
        body(k)
        return carry

    lax.fori_loop(0, count, step, 0)


def tile(t):
    return pl.ds(pl.multiple_of(t * COLS, 128), COLS)


def wide(t):
    return pl.ds(pl.multiple_of(t * WIDE, 128), WIDE)


def strip(i):
    return pl.ds(pl.multiple_of(i * ROWS, ROWS), ROWS)


def step_kernel(
    wiring_ref, gain_ref, own_any, down_any, up_any,
    ends_ref, dgrad_ref, ugrad_ref,
    own, down, up, pieces, pieces_h, picked, hid, normed, ins, gain_out, gain_in, norm_in, norm1,
    sq_out, sq0_in, sg_slots, back_in, sg_in, sg_pick, sqf, gaf, gathered, bnd,
    ga_out, ga0_in, act_ref, gsq_ref, inv_ref, part_d, part_u, small_d, small_d1, small_u, small_u1,
    acc_d, acc_u, slab, slab_in, table_v, table,
    load, send, recv, go,
):
    s = lax.axis_index("section")
    p = lax.axis_index("peer")
    first, second = s == 0, s == 1
    my_i, my_j = place(p)
    my_stage = my_i // GROUPS
    early, late = my_stage == 0, my_stage == 1
    my_rows, my_cols = strip(my_i), tile(my_j)

    def push(src, dst, kind, section, peer, out=None):
        pltpu.make_async_remote_copy(
            src_ref=src, dst_ref=dst, send_sem=send.at[kind if out is None else out], recv_sem=recv.at[kind],
            device_id={"section": section, "peer": peer}, device_id_type=MESH,
        ).start()

    def push_or_keep(src, dst, kind, peer, out=None, section=None):
        there = s if section is None else section
        here = (peer == p) & (there == s)

        @pl.when(jnp.logical_not(here))
        def _():
            push(src, dst, kind, there, peer, out)

        @pl.when(here)
        def _():
            pltpu.make_async_copy(src, dst, recv.at[kind]).start()

    def arrived(kind, ref):
        pltpu.make_async_copy(ref, ref, recv.at[kind]).wait()

    def left(kind, ref):
        pltpu.make_async_copy(ref, ref, send.at[kind]).wait()

    own_load = pltpu.make_async_copy(own_any.at[0], own, load.at[OWN])
    down_load = pltpu.make_async_copy(down_any.at[0, 0], down, load.at[DOWN_W])
    up_load = pltpu.make_async_copy(up_any.at[0, 0], up, load.at[UP_W])
    table_load = pltpu.make_async_copy(table_v, table, load.at[TABLE])
    own_load.start()
    down_load.start()
    up_load.start()

    barrier = pltpu.get_barrier_semaphore()

    def greet(k):
        t = target(p, k)
        pl.semaphore_signal(barrier, inc=1, device_id={"section": 1 - s, "peer": t}, device_id_type=MESH)

        @pl.when(t != p)
        def _():
            pl.semaphore_signal(barrier, inc=1, device_id={"section": s, "peer": t}, device_id_type=MESH)

    loop(N, greet)

    def all_here():
        pl.semaphore_wait(barrier, 2 * N - 1)

    def make_table():
        lane = lax.broadcasted_iota(jnp.int32, (N, N), 1)
        line = lax.broadcasted_iota(jnp.int32, (N, N), 0)
        wired = jnp.broadcast_to(wiring_ref[...], (N, N))
        goes = wired == line
        earliest = jnp.min(jnp.where(goes, lane, N), axis=1, keepdims=True)
        latest = jnp.max(jnp.where(goes, lane, -1), axis=1, keepdims=True)
        mine = jnp.max(jnp.where(lane == line, wired, 0), axis=1, keepdims=True)
        again = jnp.max(jnp.where((wired == mine) & (lane < line), 1, 0), axis=1, keepdims=True)
        column = lax.broadcasted_iota(jnp.int32, (N, 128), 1)
        table_v[...] = jnp.where(
            column == 0,
            jnp.where(earliest == N, 0, earliest),
            jnp.where(column == 1, jnp.maximum(latest, 0), 2 * mine + again),
        )
        table_load.start()

    def choose(first_slot, source, q):
        picked[q, first_slot] = source[table[q, 0]]
        picked[q, first_slot + 1] = source[table[q, 1]]

    def scale():
        arrived(GAIN, gain_in)

        def one(t):
            g = gain_in[lax.div(table[t, 2], 2)]
            for c in range(COLS // 128):
                cols = pl.ds(128 * c, 128)
                norm1[t, :, cols] = (pieces_h[t, :, cols].astype(F32) * g[c : c + 1, :]).astype(BF)

        loop(N, one)

    def send_home(stage):
        arrived(BACK, back_in)

        def home(k):
            t = target(p, k)
            gathered[t] = back_in[table[t, 2]]
            push_or_keep(gathered.at[t], bnd.at[my_rows, my_cols], BND0 + stage, t, BND0, section=0)

        loop(N, home)

        @pl.when(lax.rem(my_j, 2) == 0)
        def _():
            arrived(SG, sg_in)

            def choose_sg(t):
                sg_pick[t] = sg_in[table[t, 2]]

            loop(N, choose_sg)
            c = lax.rem(my_j // 2, 2)

            @pl.when(my_j < 4)
            def _():
                loop(WAYS, lambda j: push_or_keep(sg_pick, sqf.at[c], SQF, holder(my_i, j), section=0))

            @pl.when(my_j >= 4)
            def _():
                loop(WAYS, lambda j: push(sg_pick, gaf.at[c], GAF, 1 - stage, holder(my_i, j)))

        def home1(k):
            t = target(p, k)
            push_or_keep(gathered.at[t], ends_ref.at[0, my_rows, my_cols], BND1, t, section=1)

        loop(N, home1)

    def up0():
        arrived(SQ0, sq0_in)
        partial(small_u, part_u, some_rows(sq0_in), some_rows(gathered))
        send_up(small_u, UPA)

    def middle(act, gsq):
        sig = jax.nn.sigmoid(act)
        squashed = (act * sig).astype(BF)
        ga = (gsq * sig * (1.0 + act * (1.0 - sig))).astype(BF)
        return squashed, ga

    def some_rows(ref):
        return lambda t: ref[pl.ds(t * 16, 16)].reshape(16 * ROWS, ref.shape[2])

    def some_chunks(ref):
        def rows(t):
            at = pl.ds(t * 16, 16)
            return jnp.concatenate([ref[c, at].reshape(16 * ROWS, CHUNK) for c in range(2)], axis=1)

        return rows

    def partial(small, out, left_of, right_of):
        out[...] = jnp.zeros_like(out)

        def some(t):
            out[...] += tn(left_of(t), right_of(t))

        loop(4, some)
        small[...] = out[...].astype(BF)

    def send_up(part, kind):
        def one(i):
            src = part.at[pl.ds(pl.multiple_of(i * 32, 32), 32)]
            dst = acc_u.at[my_i]
            peer = holder(i, my_j)
            if kind == UPA:
                push_or_keep(src, dst, kind, peer, section=0)
            else:
                push(src, dst, kind, 1, peer)

        loop(WAYS, one)

    def send_down(part, kind, section):
        def one(r):
            src = part.at[pl.ds(pl.multiple_of(r * 80, 16), 80)]
            push_or_keep(src, acc_d.at[my_i], kind, my_j * WAYS + r, section=section)

        loop(WAYS, one)

    def down1():
        arrived(GAF, gaf)
        partial(small_d1, part_d, some_rows(norm1), some_chunks(gaf))
        send_down(small_d1, DOWN1, 1)

    def left_chunks(sender, count):
        even = (lax.rem(my_j, 2) == 0) & sender
        per_chunk = N * ROWS * CHUNK // RANK

        @pl.when(even & (my_j < 4))
        def _():
            left(SQF, down.at[pl.ds(0, count * per_chunk)])

        @pl.when(even & (my_j >= 4))
        def _():
            left(GAF, down.at[pl.ds(0, WAYS * per_chunk)])

    factor = 1.0 / math.sqrt(TOK * N)

    def total_of(acc):
        total = acc[0].astype(F32)
        for i in range(1, WAYS):
            total = total + acc[i].astype(F32)
        return total * factor

    def finish_up(kind):
        arrived(kind, acc_u)
        total = total_of(acc_u)
        for r in range(WAYS):
            slab[r, 0:4, :] = total[4 * r : 4 * r + 4, :]
        loop(WAYS, lambda r: push_or_keep(slab.at[r], slab_in.at[my_j], UPB, my_i * WAYS + r))

    def left_but_own(kind, ref, has_own):
        @pl.when(has_own)
        def _():
            left(kind, ref.at[pl.ds(0, WAYS - 1)])

        @pl.when(jnp.logical_not(has_own))
        def _():
            left(kind, ref)

    def finish(kind):
        arrived(UPB, slab_in)
        for j in range(WAYS):
            ugrad_ref[0, :, COLS * j : COLS * (j + 1)] = slab_in[j, 0:4, :]
        arrived(kind, acc_d)
        dgrad_ref[0] = total_of(acc_d)
        left_but_own(UPB, slab, my_i == p // WAYS)

    @pl.when(first)
    def _():
        own_load.wait()

        def forward(stage):
            rows = pl.ds(stage * PART, PART)
            squares = lax.fori_loop(
                0, WIDTH // WIDE,
                lambda t, c: c + jnp.sum(jnp.square(own[rows, wide(t)].astype(F32)), axis=1, keepdims=True),
                jnp.zeros((PART, 1), F32),
            )
            inverse = lax.rsqrt(squares * (1.0 / WIDTH) + 1e-06)
            inv_ref[rows, :] = jnp.broadcast_to(inverse, (PART, 128))
            act_ref[rows, :] = jnp.zeros((PART, RANK), F32)

            if stage == 0:
                down_load.wait()

            def enter(t):
                cols = wide(t)
                v = own[rows, cols].astype(F32)
                n = (v * inverse * gain_ref[0, :, cols].astype(F32)).astype(BF)
                normed[rows, cols] = n
                act_ref[rows, :] += nn(n, down[cols, :])

            loop(WIDTH // WIDE, enter)
            act = act_ref[rows, :]
            sq_out[rows, :] = (act * jax.nn.sigmoid(act)).astype(BF)

            if stage == 0:
                up_load.wait()

            def leave(t):
                cols = wide(t)
                v = own[rows, cols].astype(F32)
                hid[rows, cols] = (v + nn(sq_out[rows, :], up[:, cols])).astype(BF)

            loop(WIDTH // WIDE, leave)

        def spread(stage):
            def one(m):
                t = mate(p, stage, m)
                i, j = place(t)
                push_or_keep(hid.at[strip(i), tile(j)], pieces_h.at[p], ENDH, t, section=1 - stage)

            loop(N // STAGES, one)

        def norms(k):
            t = target(p, k)
            i, j = place(t)
            push_or_keep(normed.at[strip(i), tile(j)], norm_in.at[p], NORM, t)

        def squashes(k):
            t = target(p, k)
            i, _ = place(t)
            push_or_keep(sq_out.at[strip(i)], sq0_in.at[p], SQ0, t, section=i // GROUPS)

        forward(0)
        all_here()
        spread(0)
        forward(1)
        spread(1)
        make_table()
        table_load.wait()

        @pl.when(early)
        def _():
            arrived(ENDS, pieces)

            def one(k, out):
                q = target(p, k)
                choose(0, pieces, q)
                push(picked.at[q, pl.ds(0, 2)], ins.at[pl.ds(2, 2), my_rows, my_cols], COT, 1, q, out)

            loop(EARLY, lambda k: one(k, COT))
            loop(N - EARLY, lambda k: one(k + EARLY, COT_LATE))
            loop(N, squashes)
            loop(N, norms)
            left(COT, picked.at[pl.ds(0, EARLY), pl.ds(0, 2)])
            pl.semaphore_signal(go, inc=1, device_id={"section": 0, "peer": p + 1}, device_id_type=MESH)

        @pl.when(late)
        def _():
            loop(N, squashes)
            pl.semaphore_wait(go, 1)
            arrived(ENDS, pieces)
            arrived(ENDH, pieces_h)

            def one(k):
                q = target(p, k)
                choose(0, pieces_h, q)
                choose(2, pieces, q)
                push(picked.at[q], ins.at[:, my_rows, my_cols], BOTH, 1, q)

            loop(N, one)
            scale()
            left(BOTH, picked)
            loop(N, norms)

        def up1():
            arrived(SQF, sqf)
            partial(small_u1, part_u, some_chunks(sqf), some_rows(pieces))
            send_up(small_u1, UPA1)

        def backward(stage):
            rows = pl.ds(pl.multiple_of(stage * PART, PART), PART)

            @pl.when((stage == 0) & early)
            def _():
                send_home(0)

            @pl.when(stage == 1)
            def _():
                @pl.when(early)
                def _():
                    up0()
                    up1()

            arrived(BND0 + stage, bnd.at[rows, :])
            gsq_ref[rows, :] = jnp.zeros((PART, RANK), F32)

            def into(t):
                cols = wide(t)
                gsq_ref[rows, :] += nt(bnd[rows, cols], up[:, cols])

            loop(WIDTH // WIDE, into)
            act = act_ref[rows, :]
            _, ga = middle(act, gsq_ref[rows, :])
            ga_out[rows, :] = ga

            def give(m):
                t = mate(p, stage, m)
                i, _ = place(t)
                push_or_keep(ga_out.at[strip(i)], ga0_in.at[p], GA0, t)

            loop(N // STAGES, give)
            inverse = inv_ref[rows, 0:1]
            dots = jnp.sum(ga.astype(F32) * act, axis=1, keepdims=True) * (1.0 / WIDTH)
            pull = inverse * inverse * dots

            def out(t):
                cols = wide(t)
                gn = nt(ga_out[rows, :], down[cols, :]) * gain_ref[0, :, cols].astype(F32)
                v = own[rows, cols].astype(F32)
                ends_ref[0, rows, cols] = (bnd[rows, cols].astype(F32) + inverse * gn - v * pull).astype(BF)

            loop(WIDTH // WIDE, out)

        loop(STAGES, backward)

        @pl.when(late)
        def _():
            up1()
            down1()

        arrived(NORM, norm_in)
        arrived(GA0, ga0_in)
        partial(small_d, part_d, some_rows(norm_in), some_rows(ga0_in))
        send_down(small_d, DOWN, 0)
        finish_up(UPA)
        finish(DOWN)
        left_but_own(DOWN, acc_d, my_j == p // WAYS)
        left(NORM, norm_in.at[pl.ds(0, N - 1)])
        left(GA0, ga0_in.at[pl.ds(0, N - 1)])
        left(UPA1, acc_u)

        @pl.when(early)
        def _():
            left(ENDH, pieces_h)
            left(SQ0, sq0_in.at[pl.ds(0, N - 1)])
            left(BND0, gathered.at[pl.ds(0, N - 1)])
            left(BND1, gathered)
            left(UPA, acc_u.at[pl.ds(0, WAYS - 1)])
            left(COT_LATE, picked.at[pl.ds(0, N - EARLY), pl.ds(0, 2)])

        @pl.when(late)
        def _():
            left(ENDH, pieces_h.at[pl.ds(0, N - 1)])
            left(SQ0, sq0_in)
            left(DOWN1, acc_d)

        left_chunks(early, WAYS - 1)

    @pl.when(second)
    def _():
        own_load.wait()
        all_here()

        def spread(stage):
            def one(m):
                t = mate(p, stage, m)
                i, j = place(t)
                push(own.at[strip(i), tile(j)], pieces.at[p], ENDS, 0, t)

            loop(N // STAGES, one)

        loop(STAGES, spread)
        for j in range(WAYS):
            for c in range(COLS // 128):
                at = COLS * j + 128 * c
                gain_out[j, c : c + 1, :] = gain_ref[0, :, at : at + 128].astype(F32)

        def gains(k):
            t = target(p, k)
            i, j = place(t)
            push_or_keep(gain_out.at[j], gain_in.at[p], GAIN, t, section=1 - i // GROUPS)

        loop(N, gains)
        down_load.wait()
        up_load.wait()
        make_table()
        table_load.wait()

        @pl.when(early)
        def _():
            arrived(ENDH, pieces_h)

            def one(k):
                q = target(p, k)
                choose(0, pieces_h, q)
                push_or_keep(
                    picked.at[q, pl.ds(0, 2)], ins.at[pl.ds(0, 2), my_rows, my_cols], HID, q
                )

            loop(N, one)
            scale()

        both = 2 * PART

        def through(stage):
            rows = pl.ds(pl.multiple_of(stage * PART, PART), PART)

            @pl.when(stage == 0)
            def _():
                arrived(HID, ins.at[pl.ds(0, 2), rows, :])
                arrived(COT, ins.at[pl.ds(2, 2), rows, :])

            @pl.when(stage == 1)
            def _():
                arrived(BOTH, ins.at[:, rows, :])

            squares = lax.fori_loop(
                0, WIDTH // WIDE,
                lambda t, c: c
                + jnp.sum(jnp.square(ins[0:2, rows, wide(t)].reshape(both, WIDE).astype(F32)), axis=1, keepdims=True),
                jnp.zeros((both, 1), F32),
            )
            inverse = lax.rsqrt(squares * (1.0 / WIDTH) + 1e-06)
            act_ref[0:both, :] = jnp.zeros((both, RANK), F32)

            def enter(t):
                cols = wide(t)
                v = ins[0:2, rows, cols].reshape(both, WIDE).astype(F32)
                n = (v * inverse * gain_ref[0, :, cols].astype(F32)).astype(BF)
                act_ref[0:both, :] += nn(n, down[cols, :])

            loop(WIDTH // WIDE, enter)
            gsq_ref[0:both, :] = jnp.zeros((both, RANK), F32)

            def into(t):
                cols = wide(t)
                gsq_ref[0:both, :] += nt(ins[2:4, rows, cols].reshape(both, WIDE), up[:, cols])

            loop(WIDTH // WIDE, into)
            act = act_ref[0:both, :]
            squashed, ga = middle(act, gsq_ref[0:both, :])
            sg_slots[:, rows, 0:RANK] = squashed.reshape(2, PART, RANK)
            ga32 = ga.astype(F32)
            sg_slots[:, rows, RANK : 2 * RANK] = (ga32 * inverse).astype(BF).reshape(2, PART, RANK)
            dots = jnp.sum(ga32 * act, axis=1, keepdims=True) * (1.0 / WIDTH)
            pull = inverse * inverse * dots

            def out(t):
                u = lax.rem(t + p, WIDTH // WIDE)
                cols = wide(u)
                gn = nt(ga, down[cols, :]) * gain_ref[0, :, cols].astype(F32)
                v = ins[0:2, rows, cols].reshape(both, WIDE).astype(F32)
                c = ins[2:4, rows, cols].reshape(both, WIDE).astype(F32)
                ins[2:4, rows, cols] = (c + inverse * gn - v * pull).astype(BF).reshape(2, PART, WIDE)

                def give(n):
                    i = stage * GROUPS + lax.rem(n, GROUPS)
                    j = u * (WIDE // COLS) + n // GROUPS
                    push_or_keep(ins.at[pl.ds(2, 2), strip(i), tile(j)], back_in.at[pl.ds(2 * p, 2)], BACK, holder(i, j), section=stage)

                loop(GROUPS * WIDE // COLS, give)

            loop(WIDTH // WIDE, out)

            def extras(m):
                i = stage * GROUPS + lax.rem(m, GROUPS)
                c = m // GROUPS
                cols = pl.ds(pl.multiple_of(c * CHUNK, CHUNK), CHUNK)
                push_or_keep(sg_slots.at[:, strip(i), cols], sg_in.at[pl.ds(2 * p, 2)], SG, holder(i, 2 * c), section=stage)

            loop(GROUPS * (2 * RANK // CHUNK), extras)

        loop(STAGES, through)

        @pl.when(late)
        def _():
            send_home(1)
            up0()

        pl.when(early)(down1)
        finish_up(UPA1)
        finish(DOWN1)
        arrived(BND1, ends_ref.at[0])
        left(ENDS, pieces)

        @pl.when(early)
        def _():
            left(GAIN, gain_in.at[pl.ds(0, N - 1)])
            left(BACK, back_in)
            left(HID, picked.at[pl.ds(0, N - 1), pl.ds(0, 2)])
            left_but_own(DOWN1, acc_d, my_j == p // WAYS)

        @pl.when(late)
        def _():
            left(GAIN, gain_in)
            left(BACK, back_in.at[pl.ds(0, 2 * N - 2)])
            left(BND0, gathered)
            left(BND1, gathered.at[pl.ds(0, N - 1)])
            left(UPA, acc_u)

        own_chunk = late & (lax.rem(my_j, 2) == 0)

        @pl.when(own_chunk)
        def _():
            left(SG, sg_in.at[pl.ds(0, N - 2)])

        @pl.when(jnp.logical_not(own_chunk))
        def _():
            left(SG, sg_in.at[pl.ds(0, N)])


        left_chunks(late, WAYS)


def shards(batch_ends, wiring, down_proj, up_proj, norm_gain):
    vmem = pl.BlockSpec(memory_space=pltpu.VMEM)
    hbm = pl.BlockSpec(memory_space=pl.ANY)
    block = (TOK, WIDTH)
    scratch = [
        pltpu.VMEM(block, BF),
        pltpu.VMEM((WIDTH, RANK), BF),
        pltpu.VMEM((RANK, WIDTH), BF),
        pltpu.VMEM((N, ROWS, COLS), BF),
        pltpu.VMEM((N, ROWS, COLS), BF),
        pltpu.VMEM((N, 4, ROWS, COLS), BF),
        pltpu.VMEM(block, BF),
        pltpu.VMEM(block, BF),
        pltpu.VMEM((4, *block), BF),
        pltpu.VMEM((WAYS, 8, 128), F32),
        pltpu.VMEM((N, 8, 128), F32),
        pltpu.VMEM((N, ROWS, COLS), BF),
        pltpu.VMEM((N, ROWS, COLS), BF),
        pltpu.VMEM((TOK, RANK), BF),
        pltpu.VMEM((N, ROWS, RANK), BF),
        pltpu.VMEM((2, TOK, 2 * RANK), BF),
        pltpu.VMEM((2 * N, ROWS, COLS), BF),
        pltpu.VMEM((2 * N, ROWS, CHUNK), BF),
        pltpu.VMEM((N, ROWS, CHUNK), BF),
        pltpu.VMEM((2, N, ROWS, CHUNK), BF),
        pltpu.VMEM((2, N, ROWS, CHUNK), BF),
        pltpu.VMEM((N, ROWS, COLS), BF),
        pltpu.VMEM(block, BF),
        pltpu.VMEM((TOK, RANK), BF),
        pltpu.VMEM((N, ROWS, RANK), BF),
        pltpu.VMEM((2 * TOK, RANK), F32),
        pltpu.VMEM((2 * TOK, RANK), F32),
        pltpu.VMEM((TOK, 128), F32),
        pltpu.VMEM((COLS, RANK), F32),
        pltpu.VMEM((RANK, COLS), F32),
        pltpu.VMEM((COLS, RANK), BF),
        pltpu.VMEM((COLS, RANK), BF),
        pltpu.VMEM((RANK, COLS), BF),
        pltpu.VMEM((RANK, COLS), BF),
        pltpu.VMEM((WAYS, 80, RANK), BF),
        pltpu.VMEM((WAYS, 32, COLS), BF),
        pltpu.VMEM((WAYS, 8, COLS), F32),
        pltpu.VMEM((WAYS, 8, COLS), F32),
        pltpu.VMEM((N, 128), jnp.int32),
        pltpu.SMEM((N, 128), jnp.int32),
        pltpu.SemaphoreType.DMA((LOADS,)),
        pltpu.SemaphoreType.DMA((CLASSES,)),
        pltpu.SemaphoreType.DMA((CLASSES,)),
        pltpu.SemaphoreType.REGULAR,
    ]
    return pl.pallas_call(
        step_kernel,
        out_shape=(
            jax.ShapeDtypeStruct((1, *block), BF),
            jax.ShapeDtypeStruct((1, WIDTH // N, RANK), F32),
            jax.ShapeDtypeStruct((1, RANK // N, WIDTH), F32),
        ),
        in_specs=[vmem, vmem, hbm, hbm, hbm],
        out_specs=(vmem, vmem, vmem),
        scratch_shapes=scratch,
        compiler_params=pltpu.CompilerParams(
            collective_id=0, has_side_effects=True, vmem_limit_bytes=56 * 1024 * 1024
        ),
        name="adapter_step",
    )(wiring[None], norm_gain, batch_ends, down_proj, up_proj)


def solution(mesh):
    return jax.shard_map(
        shards,
        mesh=mesh,
        in_specs=(
            P("section", "peer", None),
            P(),
            P("section", "peer", None, None),
            P("section", "peer", None, None),
            P("section", "peer", None),
        ),
        out_specs=(
            P("section", "peer", None),
            P("section", "peer", None),
            P("section", "peer", None),
        ),
        check_vma=False,
    )
```

```python
import functools
import math

import jax
import jax.numpy as jnp
from jax import lax
from jax.experimental import pallas as pl
from jax.experimental.pallas import tpu as pltpu
from jax.sharding import PartitionSpec as P

N = 64
ROWS = 16
COLS = 640
WAYS = 8
TOK, WIDTH, RANK = 128, 5120, 256
BF, F32 = jnp.bfloat16, jnp.float32
MESH = pl.DeviceIdType.MESH

STAGES = 2
GROUPS = WAYS // STAGES
PART = TOK // STAGES
WIDE = 1280

(ENDS, ENDH, GAIN, NORM, SQ0, COT, COT_LATE, HID, BOTH, BACK, SG, SQF, GAF, BND1, GA0, DOWN, DOWN1, UPA, UPA1, UPB, BND0) = range(21)
CLASSES = 20 + STAGES
EARLY = 16
CHUNK = 128
(OWN, DOWN_W, UP_W, TABLE, LOADS) = range(5)


def target(p, k):
    a = lax.rem(lax.rem(k, 4) + 2 * lax.rem(p, 2), 4)
    b = lax.rem(k // 4, 4)
    x = lax.rem(p // 16 + a, 4)
    y = lax.rem(lax.rem(p // 4, 4) + a + b, 4)
    z = lax.rem(lax.rem(p // 2, 2) + lax.rem(k // 16, 2) + a, 2)
    core = lax.rem(lax.rem(p, 2) + k // 32 + a // 2, 2)
    return x * 16 + y * 4 + z * 2 + core


def place(k):
    m = k // 2
    return lax.rem(k, 2) * GROUPS + m // WAYS, lax.rem(m, WAYS)


def holder(i, j):
    return 2 * (lax.rem(i, GROUPS) * WAYS + j) + i // GROUPS


def mate(p, stage, m):
    a = lax.rem(lax.rem(m, 4) + 2 * lax.rem(p, 2), 4)
    b = lax.rem(m // 4, 4)
    x = lax.rem(p // 16 + a, 4)
    y = lax.rem(lax.rem(p // 4, 4) + a + b, 4)
    z = lax.rem(lax.rem(p // 2, 2) + m // 16 + a, 2)
    return x * 16 + y * 4 + z * 2 + stage


def nn(left, right):
    return jnp.dot(left, right, preferred_element_type=F32)


def nt(left, right):
    return lax.dot_general(left, right, (((1,), (1,)), ((), ())), preferred_element_type=F32)


def tn(left, right):
    return lax.dot_general(left, right, (((0,), (0,)), ((), ())), preferred_element_type=F32)


def loop(count, body):
    def step(k, carry):
        body(k)
        return carry

    lax.fori_loop(0, count, step, 0)


def tile(t):
    return pl.ds(pl.multiple_of(t * COLS, 128), COLS)


def wide(t):
    return pl.ds(pl.multiple_of(t * WIDE, 128), WIDE)


def strip(i):
    return pl.ds(pl.multiple_of(i * ROWS, ROWS), ROWS)


def step_kernel(
    wiring_ref, gain_ref, own_any, down_any, up_any,
    ends_ref, dgrad_ref, ugrad_ref,
    own, down, up, pieces, pieces_h, picked, hid, normed, ins, gain_out, gain_in, norm_in, norm1,
    sq_out, sq0_in, sg_slots, back_in, sg_in, sg_pick, sqf, gaf, gathered, bnd,
    ga_out, ga0_in, act_ref, gsq_ref, inv_ref, part_d, part_u, small_d, small_d1, small_u, small_u1,
    acc_d, acc_u, slab, slab_in, table_v, table,
    load, send, recv, go,
):
    s = lax.axis_index("section")
    p = lax.axis_index("peer")
    first, second = s == 0, s == 1
    my_i, my_j = place(p)
    my_stage = my_i // GROUPS
    early, late = my_stage == 0, my_stage == 1
    my_rows, my_cols = strip(my_i), tile(my_j)

    def push(src, dst, kind, section, peer, out=None):
        pltpu.make_async_remote_copy(
            src_ref=src, dst_ref=dst, send_sem=send.at[kind if out is None else out], recv_sem=recv.at[kind],
            device_id={"section": section, "peer": peer}, device_id_type=MESH,
        ).start()

    def push_or_keep(src, dst, kind, peer, out=None, section=None):
        there = s if section is None else section
        here = (peer == p) & (there == s)

        @pl.when(jnp.logical_not(here))
        def _():
            push(src, dst, kind, there, peer, out)

        @pl.when(here)
        def _():
            pltpu.make_async_copy(src, dst, recv.at[kind]).start()

    def arrived(kind, ref):
        pltpu.make_async_copy(ref, ref, recv.at[kind]).wait()

    def left(kind, ref):
        pltpu.make_async_copy(ref, ref, send.at[kind]).wait()

    own_load = pltpu.make_async_copy(own_any.at[0], own, load.at[OWN])
    down_load = pltpu.make_async_copy(down_any.at[0, 0], down, load.at[DOWN_W])
    up_load = pltpu.make_async_copy(up_any.at[0, 0], up, load.at[UP_W])
    table_load = pltpu.make_async_copy(table_v, table, load.at[TABLE])
    own_load.start()
    down_load.start()
    up_load.start()

    barrier = pltpu.get_barrier_semaphore()

    def greet(k):
        for n in range(7):
            t = lax.rem(p + 1 + 7 * k + n, N)
            for section in (0, 1):
                pl.semaphore_signal(barrier, inc=1, device_id={"section": section, "peer": t}, device_id_type=MESH)

    loop(9, greet)
    pl.semaphore_signal(barrier, inc=1, device_id={"section": 1 - s, "peer": p}, device_id_type=MESH)

    def all_here():
        pl.semaphore_wait(barrier, 2 * N - 1)

    def make_table():
        lane = lax.broadcasted_iota(jnp.int32, (N, N), 1)
        line = lax.broadcasted_iota(jnp.int32, (N, N), 0)
        wired = jnp.broadcast_to(wiring_ref[...], (N, N))
        goes = wired == line
        earliest = jnp.min(jnp.where(goes, lane, N), axis=1, keepdims=True)
        latest = jnp.max(jnp.where(goes, lane, -1), axis=1, keepdims=True)
        mine = jnp.max(jnp.where(lane == line, wired, 0), axis=1, keepdims=True)
        again = jnp.max(jnp.where((wired == mine) & (lane < line), 1, 0), axis=1, keepdims=True)
        column = lax.broadcasted_iota(jnp.int32, (N, 128), 1)
        table_v[...] = jnp.where(
            column == 0,
            jnp.where(earliest == N, 0, earliest),
            jnp.where(column == 1, jnp.maximum(latest, 0), 2 * mine + again),
        )
        table_load.start()

    def choose(first_slot, source, q):
        picked[q, first_slot] = source[table[q, 0]]
        picked[q, first_slot + 1] = source[table[q, 1]]

    def scale():
        arrived(GAIN, gain_in)

        def one(t):
            g = gain_in[lax.div(table[t, 2], 2)]
            for c in range(COLS // 128):
                cols = pl.ds(128 * c, 128)
                norm1[t, :, cols] = (pieces_h[t, :, cols].astype(F32) * g[c : c + 1, :]).astype(BF)

        loop(N, one)

    def send_home(stage):
        arrived(BACK, back_in)

        def home(k):
            t = target(p, k)
            gathered[t] = back_in[table[t, 2]]
            push_or_keep(gathered.at[t], bnd.at[my_rows, my_cols], BND0 + stage, t, BND0, section=0)

        loop(N, home)

        @pl.when(lax.rem(my_j, 2) == 0)
        def _():
            arrived(SG, sg_in)

            def choose_sg(t):
                sg_pick[t] = sg_in[table[t, 2]]

            loop(N, choose_sg)
            c = lax.rem(my_j // 2, 2)

            @pl.when(my_j < 4)
            def _():
                loop(WAYS, lambda j: push_or_keep(sg_pick, sqf.at[c], SQF, holder(my_i, j), section=0))

            @pl.when(my_j >= 4)
            def _():
                loop(WAYS, lambda j: push(sg_pick, gaf.at[c], GAF, 1 - stage, holder(my_i, j)))

        def home1(k):
            t = target(p, k)
            push_or_keep(gathered.at[t], ends_ref.at[0, my_rows, my_cols], BND1, t, section=1)

        loop(N, home1)

    def up0():
        arrived(SQ0, sq0_in)
        partial(small_u, part_u, some_rows(sq0_in), some_rows(gathered))
        send_up(small_u, UPA)

    def middle(act, gsq):
        sig = jax.nn.sigmoid(act)
        squashed = (act * sig).astype(BF)
        ga = (gsq * sig * (1.0 + act * (1.0 - sig))).astype(BF)
        return squashed, ga

    def some_rows(ref):
        return lambda t: ref[pl.ds(t * 16, 16)].reshape(16 * ROWS, ref.shape[2])

    def some_chunks(ref):
        def rows(t):
            at = pl.ds(t * 16, 16)
            return jnp.concatenate([ref[c, at].reshape(16 * ROWS, CHUNK) for c in range(2)], axis=1)

        return rows

    def partial(small, out, left_of, right_of):
        out[...] = jnp.zeros_like(out)

        def some(t):
            out[...] += tn(left_of(t), right_of(t))

        loop(4, some)
        small[...] = out[...].astype(BF)

    def send_up(part, kind):
        def one(i):
            src = part.at[pl.ds(pl.multiple_of(i * 32, 32), 32)]
            dst = acc_u.at[my_i]
            peer = holder(i, my_j)
            if kind == UPA:
                push_or_keep(src, dst, kind, peer, section=0)
            else:
                push(src, dst, kind, 1, peer)

        loop(WAYS, one)

    def send_down(part, kind, section):
        def one(r):
            src = part.at[pl.ds(pl.multiple_of(r * 80, 16), 80)]
            push_or_keep(src, acc_d.at[my_i], kind, my_j * WAYS + r, section=section)

        loop(WAYS, one)

    def down1():
        arrived(GAF, gaf)
        partial(small_d1, part_d, some_rows(norm1), some_chunks(gaf))
        send_down(small_d1, DOWN1, 1)

    def left_chunks(sender, count):
        even = (lax.rem(my_j, 2) == 0) & sender
        per_chunk = N * ROWS * CHUNK // RANK

        @pl.when(even & (my_j < 4))
        def _():
            left(SQF, down.at[pl.ds(0, count * per_chunk)])

        @pl.when(even & (my_j >= 4))
        def _():
            left(GAF, down.at[pl.ds(0, WAYS * per_chunk)])

    factor = 1.0 / math.sqrt(TOK * N)

    def total_of(acc):
        total = acc[0].astype(F32)
        for i in range(1, WAYS):
            total = total + acc[i].astype(F32)
        return total * factor

    def finish_up(kind):
        arrived(kind, acc_u)
        total = total_of(acc_u)
        for r in range(WAYS):
            slab[r, 0:4, :] = total[4 * r : 4 * r + 4, :]
        loop(WAYS, lambda r: push_or_keep(slab.at[r], slab_in.at[my_j], UPB, my_i * WAYS + r))

    def left_but_own(kind, ref, has_own):
        @pl.when(has_own)
        def _():
            left(kind, ref.at[pl.ds(0, WAYS - 1)])

        @pl.when(jnp.logical_not(has_own))
        def _():
            left(kind, ref)

    def finish(kind):
        arrived(UPB, slab_in)
        for j in range(WAYS):
            ugrad_ref[0, :, COLS * j : COLS * (j + 1)] = slab_in[j, 0:4, :]
        arrived(kind, acc_d)
        dgrad_ref[0] = total_of(acc_d)
        left_but_own(UPB, slab, my_i == p // WAYS)

    @pl.when(first)
    def _():
        own_load.wait()

        def forward(stage):
            rows = pl.ds(stage * PART, PART)
            squares = lax.fori_loop(
                0, WIDTH // WIDE,
                lambda t, c: c + jnp.sum(jnp.square(own[rows, wide(t)].astype(F32)), axis=1, keepdims=True),
                jnp.zeros((PART, 1), F32),
            )
            inverse = lax.rsqrt(squares * (1.0 / WIDTH) + 1e-06)
            inv_ref[rows, :] = jnp.broadcast_to(inverse, (PART, 128))
            act_ref[rows, :] = jnp.zeros((PART, RANK), F32)

            if stage == 0:
                down_load.wait()

            def enter(t):
                cols = wide(t)
                v = own[rows, cols].astype(F32)
                n = (v * inverse * gain_ref[0, :, cols].astype(F32)).astype(BF)
                normed[rows, cols] = n
                act_ref[rows, :] += nn(n, down[cols, :])

            loop(WIDTH // WIDE, enter)
            act = act_ref[rows, :]
            sq_out[rows, :] = (act * jax.nn.sigmoid(act)).astype(BF)

            if stage == 0:
                up_load.wait()

            def leave(t):
                cols = wide(t)
                v = own[rows, cols].astype(F32)
                hid[rows, cols] = (v + nn(sq_out[rows, :], up[:, cols])).astype(BF)

            loop(WIDTH // WIDE, leave)

        def spread(stage):
            def one(m):
                t = mate(p, stage, m)
                i, j = place(t)
                push_or_keep(hid.at[strip(i), tile(j)], pieces_h.at[p], ENDH, t, section=1 - stage)

            loop(N // STAGES, one)

        def norms(k):
            t = target(p, k)
            i, j = place(t)
            push_or_keep(normed.at[strip(i), tile(j)], norm_in.at[p], NORM, t)

        def squashes(k):
            t = target(p, k)
            i, _ = place(t)
            push_or_keep(sq_out.at[strip(i)], sq0_in.at[p], SQ0, t, section=i // GROUPS)

        forward(0)
        all_here()
        spread(0)
        forward(1)
        spread(1)
        make_table()
        table_load.wait()

        @pl.when(early)
        def _():
            arrived(ENDS, pieces)

            def one(k, out):
                q = target(p, k)
                choose(0, pieces, q)
                push(picked.at[q, pl.ds(0, 2)], ins.at[pl.ds(2, 2), my_rows, my_cols], COT, 1, q, out)

            loop(EARLY, lambda k: one(k, COT))
            loop(N - EARLY, lambda k: one(k + EARLY, COT_LATE))
            loop(N, squashes)
            loop(N, norms)
            pl.semaphore_signal(go, inc=1, device_id={"section": 0, "peer": p + 1}, device_id_type=MESH)
            left(COT, picked.at[pl.ds(0, EARLY), pl.ds(0, 2)])

        @pl.when(late)
        def _():
            loop(N, squashes)
            pl.semaphore_wait(go, 1)
            arrived(ENDS, pieces)
            arrived(ENDH, pieces_h)

            def one(k):
                q = target(p, k)
                choose(0, pieces_h, q)
                choose(2, pieces, q)
                push(picked.at[q], ins.at[:, my_rows, my_cols], BOTH, 1, q)

            loop(N, one)
            scale()
            left(BOTH, picked)
            loop(N, norms)

        def up1():
            arrived(SQF, sqf)
            partial(small_u1, part_u, some_chunks(sqf), some_rows(pieces))
            send_up(small_u1, UPA1)

        def backward(stage):
            rows = pl.ds(pl.multiple_of(stage * PART, PART), PART)

            @pl.when((stage == 0) & early)
            def _():
                send_home(0)

            @pl.when(stage == 1)
            def _():
                @pl.when(early)
                def _():
                    up0()
                    up1()

            arrived(BND0 + stage, bnd.at[rows, :])
            gsq_ref[rows, :] = jnp.zeros((PART, RANK), F32)

            def into(t):
                cols = wide(t)
                gsq_ref[rows, :] += nt(bnd[rows, cols], up[:, cols])

            loop(WIDTH // WIDE, into)
            act = act_ref[rows, :]
            _, ga = middle(act, gsq_ref[rows, :])
            ga_out[rows, :] = ga

            def give(m):
                t = mate(p, stage, m)
                i, _ = place(t)
                push_or_keep(ga_out.at[strip(i)], ga0_in.at[p], GA0, t)

            loop(N // STAGES, give)
            inverse = inv_ref[rows, 0:1]
            dots = jnp.sum(ga.astype(F32) * act, axis=1, keepdims=True) * (1.0 / WIDTH)
            pull = inverse * inverse * dots

            def out(t):
                cols = wide(t)
                gn = nt(ga_out[rows, :], down[cols, :]) * gain_ref[0, :, cols].astype(F32)
                v = own[rows, cols].astype(F32)
                ends_ref[0, rows, cols] = (bnd[rows, cols].astype(F32) + inverse * gn - v * pull).astype(BF)

            loop(WIDTH // WIDE, out)

        loop(STAGES, backward)

        arrived(NORM, norm_in)
        arrived(GA0, ga0_in)
        partial(small_d, part_d, some_rows(norm_in), some_rows(ga0_in))
        send_down(small_d, DOWN, 0)
        finish_up(UPA)

        @pl.when(late)
        def _():
            up1()
            down1()

        finish(DOWN)
        left_but_own(DOWN, acc_d, my_j == p // WAYS)
        left(NORM, norm_in.at[pl.ds(0, N - 1)])
        left(GA0, ga0_in.at[pl.ds(0, N - 1)])
        left(UPA1, acc_u)

        @pl.when(early)
        def _():
            left(ENDH, pieces_h)
            left(SQ0, sq0_in.at[pl.ds(0, N - 1)])
            left(BND0, gathered.at[pl.ds(0, N - 1)])
            left(BND1, gathered)
            left(UPA, acc_u.at[pl.ds(0, WAYS - 1)])
            left(COT_LATE, picked.at[pl.ds(0, N - EARLY), pl.ds(0, 2)])

        @pl.when(late)
        def _():
            left(ENDH, pieces_h.at[pl.ds(0, N - 1)])
            left(SQ0, sq0_in)
            left(DOWN1, acc_d)

        left_chunks(early, WAYS - 1)

    @pl.when(second)
    def _():
        own_load.wait()
        all_here()

        def spread(stage):
            def one(m):
                t = mate(p, stage, m)
                i, j = place(t)
                push(own.at[strip(i), tile(j)], pieces.at[p], ENDS, 0, t)

            loop(N // STAGES, one)

        loop(STAGES, spread)
        for j in range(WAYS):
            for c in range(COLS // 128):
                at = COLS * j + 128 * c
                gain_out[j, c : c + 1, :] = gain_ref[0, :, at : at + 128].astype(F32)

        def gains(k):
            t = target(p, k)
            i, j = place(t)
            push_or_keep(gain_out.at[j], gain_in.at[p], GAIN, t, section=1 - i // GROUPS)

        loop(N, gains)
        down_load.wait()
        up_load.wait()
        make_table()
        table_load.wait()

        @pl.when(early)
        def _():
            arrived(ENDH, pieces_h)

            def one(k):
                q = target(p, k)
                choose(0, pieces_h, q)
                push_or_keep(
                    picked.at[q, pl.ds(0, 2)], ins.at[pl.ds(0, 2), my_rows, my_cols], HID, q
                )

            loop(N, one)
            scale()

        both = 2 * PART

        def through(stage):
            rows = pl.ds(pl.multiple_of(stage * PART, PART), PART)

            @pl.when(stage == 0)
            def _():
                arrived(HID, ins.at[pl.ds(0, 2), rows, :])
                arrived(COT, ins.at[pl.ds(2, 2), rows, :])

            @pl.when(stage == 1)
            def _():
                arrived(BOTH, ins.at[:, rows, :])

            squares = lax.fori_loop(
                0, WIDTH // WIDE,
                lambda t, c: c
                + jnp.sum(jnp.square(ins[0:2, rows, wide(t)].reshape(both, WIDE).astype(F32)), axis=1, keepdims=True),
                jnp.zeros((both, 1), F32),
            )
            inverse = lax.rsqrt(squares * (1.0 / WIDTH) + 1e-06)
            act_ref[0:both, :] = jnp.zeros((both, RANK), F32)

            def enter(t):
                cols = wide(t)
                v = ins[0:2, rows, cols].reshape(both, WIDE).astype(F32)
                n = (v * inverse * gain_ref[0, :, cols].astype(F32)).astype(BF)
                act_ref[0:both, :] += nn(n, down[cols, :])

            loop(WIDTH // WIDE, enter)
            gsq_ref[0:both, :] = jnp.zeros((both, RANK), F32)

            def into(t):
                cols = wide(t)
                gsq_ref[0:both, :] += nt(ins[2:4, rows, cols].reshape(both, WIDE), up[:, cols])

            loop(WIDTH // WIDE, into)
            act = act_ref[0:both, :]
            squashed, ga = middle(act, gsq_ref[0:both, :])
            sg_slots[:, rows, 0:RANK] = squashed.reshape(2, PART, RANK)
            ga32 = ga.astype(F32)
            sg_slots[:, rows, RANK : 2 * RANK] = (ga32 * inverse).astype(BF).reshape(2, PART, RANK)
            dots = jnp.sum(ga32 * act, axis=1, keepdims=True) * (1.0 / WIDTH)
            pull = inverse * inverse * dots

            def out(t):
                u = lax.rem(t + p + p // 4 + p // 16, WIDTH // WIDE)
                cols = wide(u)
                gn = nt(ga, down[cols, :]) * gain_ref[0, :, cols].astype(F32)
                v = ins[0:2, rows, cols].reshape(both, WIDE).astype(F32)
                c = ins[2:4, rows, cols].reshape(both, WIDE).astype(F32)
                ins[2:4, rows, cols] = (c + inverse * gn - v * pull).astype(BF).reshape(2, PART, WIDE)

                def give(n):
                    i = stage * GROUPS + lax.rem(n, GROUPS)
                    j = u * (WIDE // COLS) + n // GROUPS
                    push_or_keep(ins.at[pl.ds(2, 2), strip(i), tile(j)], back_in.at[pl.ds(2 * p, 2)], BACK, holder(i, j), section=stage)

                loop(GROUPS * WIDE // COLS, give)

            loop(WIDTH // WIDE, out)

            def extras(m):
                i = stage * GROUPS + lax.rem(m, GROUPS)
                c = m // GROUPS
                cols = pl.ds(pl.multiple_of(c * CHUNK, CHUNK), CHUNK)
                push_or_keep(sg_slots.at[:, strip(i), cols], sg_in.at[pl.ds(2 * p, 2)], SG, holder(i, 2 * c), section=stage)

            loop(GROUPS * (2 * RANK // CHUNK), extras)

        loop(STAGES, through)

        @pl.when(late)
        def _():
            send_home(1)
            up0()

        pl.when(early)(down1)
        finish_up(UPA1)
        finish(DOWN1)
        arrived(BND1, ends_ref.at[0])
        left(ENDS, pieces)

        @pl.when(early)
        def _():
            left(GAIN, gain_in.at[pl.ds(0, N - 1)])
            left(BACK, back_in)
            left(HID, picked.at[pl.ds(0, N - 1), pl.ds(0, 2)])
            left_but_own(DOWN1, acc_d, my_j == p // WAYS)

        @pl.when(late)
        def _():
            left(GAIN, gain_in)
            left(BACK, back_in.at[pl.ds(0, 2 * N - 2)])
            left(BND0, gathered)
            left(BND1, gathered.at[pl.ds(0, N - 1)])
            left(UPA, acc_u)

        own_chunk = late & (lax.rem(my_j, 2) == 0)

        @pl.when(own_chunk)
        def _():
            left(SG, sg_in.at[pl.ds(0, N - 2)])

        @pl.when(jnp.logical_not(own_chunk))
        def _():
            left(SG, sg_in.at[pl.ds(0, N)])


        left_chunks(late, WAYS)


def shards(batch_ends, wiring, down_proj, up_proj, norm_gain):
    vmem = pl.BlockSpec(memory_space=pltpu.VMEM)
    hbm = pl.BlockSpec(memory_space=pl.ANY)
    block = (TOK, WIDTH)
    scratch = [
        pltpu.VMEM(block, BF),
        pltpu.VMEM((WIDTH, RANK), BF),
        pltpu.VMEM((RANK, WIDTH), BF),
        pltpu.VMEM((N, ROWS, COLS), BF),
        pltpu.VMEM((N, ROWS, COLS), BF),
        pltpu.VMEM((N, 4, ROWS, COLS), BF),
        pltpu.VMEM(block, BF),
        pltpu.VMEM(block, BF),
        pltpu.VMEM((4, *block), BF),
        pltpu.VMEM((WAYS, 8, 128), F32),
        pltpu.VMEM((N, 8, 128), F32),
        pltpu.VMEM((N, ROWS, COLS), BF),
        pltpu.VMEM((N, ROWS, COLS), BF),
        pltpu.VMEM((TOK, RANK), BF),
        pltpu.VMEM((N, ROWS, RANK), BF),
        pltpu.VMEM((2, TOK, 2 * RANK), BF),
        pltpu.VMEM((2 * N, ROWS, COLS), BF),
        pltpu.VMEM((2 * N, ROWS, CHUNK), BF),
        pltpu.VMEM((N, ROWS, CHUNK), BF),
        pltpu.VMEM((2, N, ROWS, CHUNK), BF),
        pltpu.VMEM((2, N, ROWS, CHUNK), BF),
        pltpu.VMEM((N, ROWS, COLS), BF),
        pltpu.VMEM(block, BF),
        pltpu.VMEM((TOK, RANK), BF),
        pltpu.VMEM((N, ROWS, RANK), BF),
        pltpu.VMEM((2 * TOK, RANK), F32),
        pltpu.VMEM((2 * TOK, RANK), F32),
        pltpu.VMEM((TOK, 128), F32),
        pltpu.VMEM((COLS, RANK), F32),
        pltpu.VMEM((RANK, COLS), F32),
        pltpu.VMEM((COLS, RANK), BF),
        pltpu.VMEM((COLS, RANK), BF),
        pltpu.VMEM((RANK, COLS), BF),
        pltpu.VMEM((RANK, COLS), BF),
        pltpu.VMEM((WAYS, 80, RANK), BF),
        pltpu.VMEM((WAYS, 32, COLS), BF),
        pltpu.VMEM((WAYS, 8, COLS), F32),
        pltpu.VMEM((WAYS, 8, COLS), F32),
        pltpu.VMEM((N, 128), jnp.int32),
        pltpu.SMEM((N, 128), jnp.int32),
        pltpu.SemaphoreType.DMA((LOADS,)),
        pltpu.SemaphoreType.DMA((CLASSES,)),
        pltpu.SemaphoreType.DMA((CLASSES,)),
        pltpu.SemaphoreType.REGULAR,
    ]
    return pl.pallas_call(
        step_kernel,
        out_shape=(
            jax.ShapeDtypeStruct((1, *block), BF),
            jax.ShapeDtypeStruct((1, WIDTH // N, RANK), F32),
            jax.ShapeDtypeStruct((1, RANK // N, WIDTH), F32),
        ),
        in_specs=[vmem, vmem, hbm, hbm, hbm],
        out_specs=(vmem, vmem, vmem),
        scratch_shapes=scratch,
        compiler_params=pltpu.CompilerParams(
            collective_id=0, has_side_effects=True, vmem_limit_bytes=56 * 1024 * 1024
        ),
        name="adapter_step",
    )(wiring[None], norm_gain, batch_ends, down_proj, up_proj)


def solution(mesh):
    return jax.shard_map(
        shards,
        mesh=mesh,
        in_specs=(
            P("section", "peer", None),
            P(),
            P("section", "peer", None, None),
            P("section", "peer", None, None),
            P("section", "peer", None),
        ),
        out_specs=(
            P("section", "peer", None),
            P("section", "peer", None),
            P("section", "peer", None),
        ),
        check_vma=False,
    )
```

```python
import functools
import math

import jax
import jax.numpy as jnp
from jax import lax
from jax.experimental import pallas as pl
from jax.experimental.pallas import tpu as pltpu
from jax.sharding import PartitionSpec as P

N = 64
ROWS = 16
COLS = 640
WAYS = 8
TOK, WIDTH, RANK = 128, 5120, 256
BF, F32 = jnp.bfloat16, jnp.float32
MESH = pl.DeviceIdType.MESH

STAGES = 2
GROUPS = WAYS // STAGES
PART = TOK // STAGES
WIDE = 1280

(ENDS, ENDH, GAIN, NORM, SQ0, COT, COT_LATE, HID, BOTH, BACK, SG, SQF, GAF, BND1, GA0, DOWN, DOWN1, UPA, UPA1, UPB, BND0) = range(21)
CLASSES = 20 + STAGES
EARLY = 16
CHUNK = 128
(OWN, DOWN_W, UP_W, TABLE, ENDS_OUT) = range(5)
LOADS = ENDS_OUT + STAGES


def target(p, k):
    a = lax.rem(lax.rem(k, 4) + 2 * lax.rem(p, 2), 4)
    b = lax.rem(k // 4, 4)
    x = lax.rem(p // 16 + a, 4)
    y = lax.rem(lax.rem(p // 4, 4) + a + b, 4)
    z = lax.rem(lax.rem(p // 2, 2) + lax.rem(k // 16, 2) + a, 2)
    core = lax.rem(lax.rem(p, 2) + k // 32 + a // 2, 2)
    return x * 16 + y * 4 + z * 2 + core


def place(k):
    m = k // 2
    return lax.rem(k, 2) * GROUPS + m // WAYS, lax.rem(m, WAYS)


def holder(i, j):
    return 2 * (lax.rem(i, GROUPS) * WAYS + j) + i // GROUPS


def mate(p, stage, m):
    a = lax.rem(lax.rem(m, 4) + 2 * lax.rem(p, 2), 4)
    b = lax.rem(m // 4, 4)
    x = lax.rem(p // 16 + a, 4)
    y = lax.rem(lax.rem(p // 4, 4) + a + b, 4)
    z = lax.rem(lax.rem(p // 2, 2) + m // 16 + a, 2)
    return x * 16 + y * 4 + z * 2 + stage


def nn(left, right):
    return jnp.dot(left, right, preferred_element_type=F32)


def nt(left, right):
    return lax.dot_general(left, right, (((1,), (1,)), ((), ())), preferred_element_type=F32)


def tn(left, right):
    return lax.dot_general(left, right, (((0,), (0,)), ((), ())), preferred_element_type=F32)


def loop(count, body):
    def step(k, carry):
        body(k)
        return carry

    lax.fori_loop(0, count, step, 0)


def tile(t):
    return pl.ds(pl.multiple_of(t * COLS, 128), COLS)


def wide(t):
    return pl.ds(pl.multiple_of(t * WIDE, 128), WIDE)


def strip(i):
    return pl.ds(pl.multiple_of(i * ROWS, ROWS), ROWS)


def step_kernel(
    wiring_ref, gain_ref, own_any, down_any, up_any,
    ends_ref, dgrad_ref, ugrad_ref,
    own, down, up, pieces, pieces_h, picked, hid, normed, ins, gain_out, gain_in, norm_in, norm1,
    sq_out, sq0_in, sg_slots, back_in, sg_in, sg_pick, sqf, gaf, gathered, bnd, ends_v,
    ga_out, ga0_in, act_ref, gsq_ref, inv_ref, part_d, part_u, small_d, small_d1, small_u, small_u1,
    acc_d, acc_u, slab, slab_in, table_v, table,
    load, send, recv, go,
):
    s = lax.axis_index("section")
    p = lax.axis_index("peer")
    first, second = s == 0, s == 1
    my_i, my_j = place(p)
    my_stage = my_i // GROUPS
    early, late = my_stage == 0, my_stage == 1
    my_rows, my_cols = strip(my_i), tile(my_j)

    def push(src, dst, kind, section, peer, out=None):
        pltpu.make_async_remote_copy(
            src_ref=src, dst_ref=dst, send_sem=send.at[kind if out is None else out], recv_sem=recv.at[kind],
            device_id={"section": section, "peer": peer}, device_id_type=MESH,
        ).start()

    def push_or_keep(src, dst, kind, peer, out=None, section=None):
        there = s if section is None else section
        here = (peer == p) & (there == s)

        @pl.when(jnp.logical_not(here))
        def _():
            push(src, dst, kind, there, peer, out)

        @pl.when(here)
        def _():
            pltpu.make_async_copy(src, dst, recv.at[kind]).start()

    def arrived(kind, ref):
        pltpu.make_async_copy(ref, ref, recv.at[kind]).wait()

    def left(kind, ref):
        pltpu.make_async_copy(ref, ref, send.at[kind]).wait()

    own_load = pltpu.make_async_copy(own_any.at[0], own, load.at[OWN])
    down_load = pltpu.make_async_copy(down_any.at[0, 0], down, load.at[DOWN_W])
    up_load = pltpu.make_async_copy(up_any.at[0, 0], up, load.at[UP_W])
    table_load = pltpu.make_async_copy(table_v, table, load.at[TABLE])
    own_load.start()
    down_load.start()
    up_load.start()

    barrier = pltpu.get_barrier_semaphore()

    def greet(k):
        for n in range(7):
            t = lax.rem(p + 1 + 7 * k + n, N)
            for section in (0, 1):
                pl.semaphore_signal(barrier, inc=1, device_id={"section": section, "peer": t}, device_id_type=MESH)

    loop(9, greet)
    pl.semaphore_signal(barrier, inc=1, device_id={"section": 1 - s, "peer": p}, device_id_type=MESH)

    def all_here():
        pl.semaphore_wait(barrier, 2 * N - 1)

    def make_table():
        lane = lax.broadcasted_iota(jnp.int32, (N, N), 1)
        line = lax.broadcasted_iota(jnp.int32, (N, N), 0)
        wired = jnp.broadcast_to(wiring_ref[...], (N, N))
        goes = wired == line
        earliest = jnp.min(jnp.where(goes, lane, N), axis=1, keepdims=True)
        latest = jnp.max(jnp.where(goes, lane, -1), axis=1, keepdims=True)
        mine = jnp.max(jnp.where(lane == line, wired, 0), axis=1, keepdims=True)
        again = jnp.max(jnp.where((wired == mine) & (lane < line), 1, 0), axis=1, keepdims=True)
        column = lax.broadcasted_iota(jnp.int32, (N, 128), 1)
        table_v[...] = jnp.where(
            column == 0,
            jnp.where(earliest == N, 0, earliest),
            jnp.where(column == 1, jnp.maximum(latest, 0), 2 * mine + again),
        )
        table_load.start()

    def choose(first_slot, source, q):
        picked[q, first_slot] = source[table[q, 0]]
        picked[q, first_slot + 1] = source[table[q, 1]]

    def scale():
        arrived(GAIN, gain_in)

        def one(t):
            g = gain_in[lax.div(table[t, 2], 2)]
            for c in range(COLS // 128):
                cols = pl.ds(128 * c, 128)
                norm1[t, :, cols] = (pieces_h[t, :, cols].astype(F32) * g[c : c + 1, :]).astype(BF)

        loop(N, one)

    def send_home(stage):
        arrived(BACK, back_in)

        def home(k):
            t = target(p, k)
            gathered[t] = back_in[table[t, 2]]
            push_or_keep(gathered.at[t], bnd.at[my_rows, my_cols], BND0 + stage, t, BND0, section=0)

        loop(N, home)

        @pl.when(lax.rem(my_j, 2) == 0)
        def _():
            arrived(SG, sg_in)

            def choose_sg(t):
                sg_pick[t] = sg_in[table[t, 2]]

            loop(N, choose_sg)
            c = lax.rem(my_j // 2, 2)

            @pl.when(my_j < 4)
            def _():
                loop(WAYS, lambda j: push_or_keep(sg_pick, sqf.at[c], SQF, holder(my_i, j), section=0))

            @pl.when(my_j >= 4)
            def _():
                loop(WAYS, lambda j: push(sg_pick, gaf.at[c], GAF, 1 - stage, holder(my_i, j)))

        def home1(k):
            t = target(p, k)
            push_or_keep(gathered.at[t], ends_ref.at[0, my_rows, my_cols], BND1, t, section=1)

        if stage == 1:
            up0()
        loop(N, home1)

    def up0():
        arrived(SQ0, sq0_in)
        partial(small_u, part_u, some_rows(sq0_in), some_rows(gathered))
        send_up(small_u, UPA)

    def middle(act, gsq):
        sig = jax.nn.sigmoid(act)
        squashed = (act * sig).astype(BF)
        ga = (gsq * sig * (1.0 + act * (1.0 - sig))).astype(BF)
        return squashed, ga

    def some_rows(ref):
        return lambda t: ref[pl.ds(t * 16, 16)].reshape(16 * ROWS, ref.shape[2])

    def some_chunks(ref):
        def rows(t):
            at = pl.ds(t * 16, 16)
            return jnp.concatenate([ref[c, at].reshape(16 * ROWS, CHUNK) for c in range(2)], axis=1)

        return rows

    def partial(small, out, left_of, right_of):
        out[...] = jnp.zeros_like(out)

        def some(t):
            out[...] += tn(left_of(t), right_of(t))

        loop(4, some)
        small[...] = out[...].astype(BF)

    def send_up(part, kind):
        def one(i):
            src = part.at[pl.ds(pl.multiple_of(i * 32, 32), 32)]
            dst = acc_u.at[my_i]
            peer = holder(i, my_j)
            if kind == UPA:
                push_or_keep(src, dst, kind, peer, section=0)
            else:
                push(src, dst, kind, 1, peer)

        loop(WAYS, one)

    def send_down(part, kind, section):
        def one(r):
            src = part.at[pl.ds(pl.multiple_of(r * 80, 16), 80)]
            push_or_keep(src, acc_d.at[my_i], kind, my_j * WAYS + r, section=section)

        loop(WAYS, one)

    def down1():
        arrived(GAF, gaf)
        partial(small_d1, part_d, some_rows(norm1), some_chunks(gaf))
        send_down(small_d1, DOWN1, 1)

    def left_chunks(sender, count):
        even = (lax.rem(my_j, 2) == 0) & sender
        per_chunk = N * ROWS * CHUNK // RANK

        @pl.when(even & (my_j < 4))
        def _():
            left(SQF, down.at[pl.ds(0, count * per_chunk)])

        @pl.when(even & (my_j >= 4))
        def _():
            left(GAF, down.at[pl.ds(0, WAYS * per_chunk)])

    factor = 1.0 / math.sqrt(TOK * N)

    def total_of(acc):
        total = acc[0].astype(F32)
        for i in range(1, WAYS):
            total = total + acc[i].astype(F32)
        return total * factor

    def finish_up(kind):
        arrived(kind, acc_u)
        total = total_of(acc_u)
        for r in range(WAYS):
            slab[r, 0:4, :] = total[4 * r : 4 * r + 4, :]
        loop(WAYS, lambda r: push_or_keep(slab.at[r], slab_in.at[my_j], UPB, my_i * WAYS + r))

    def left_but_own(kind, ref, has_own):
        @pl.when(has_own)
        def _():
            left(kind, ref.at[pl.ds(0, WAYS - 1)])

        @pl.when(jnp.logical_not(has_own))
        def _():
            left(kind, ref)

    def finish(kind):
        arrived(UPB, slab_in)
        for j in range(WAYS):
            ugrad_ref[0, :, COLS * j : COLS * (j + 1)] = slab_in[j, 0:4, :]
        arrived(kind, acc_d)
        dgrad_ref[0] = total_of(acc_d)
        left_but_own(UPB, slab, my_i == p // WAYS)

    @pl.when(first)
    def _():
        own_load.wait()

        def forward(stage):
            rows = pl.ds(stage * PART, PART)
            squares = lax.fori_loop(
                0, WIDTH // WIDE,
                lambda t, c: c + jnp.sum(jnp.square(own[rows, wide(t)].astype(F32)), axis=1, keepdims=True),
                jnp.zeros((PART, 1), F32),
            )
            inverse = lax.rsqrt(squares * (1.0 / WIDTH) + 1e-06)
            inv_ref[rows, :] = jnp.broadcast_to(inverse, (PART, 128))
            act_ref[rows, :] = jnp.zeros((PART, RANK), F32)

            if stage == 0:
                down_load.wait()

            def enter(t):
                cols = wide(t)
                v = own[rows, cols].astype(F32)
                n = (v * inverse * gain_ref[0, :, cols].astype(F32)).astype(BF)
                normed[rows, cols] = n
                act_ref[rows, :] += nn(n, down[cols, :])

            loop(WIDTH // WIDE, enter)
            act = act_ref[rows, :]
            sq_out[rows, :] = (act * jax.nn.sigmoid(act)).astype(BF)

            if stage == 0:
                up_load.wait()

            def leave(t):
                cols = wide(t)
                v = own[rows, cols].astype(F32)
                hid[rows, cols] = (v + nn(sq_out[rows, :], up[:, cols])).astype(BF)

            loop(WIDTH // WIDE, leave)

        def spread(stage):
            def one(m):
                t = mate(p, stage, m)
                i, j = place(t)
                push_or_keep(hid.at[strip(i), tile(j)], pieces_h.at[p], ENDH, t, section=1 - stage)

            loop(N // STAGES, one)

        def norms(k):
            t = target(p, k)
            i, j = place(t)
            push_or_keep(normed.at[strip(i), tile(j)], norm_in.at[p], NORM, t)

        def squashes(k):
            t = target(p, k)
            i, _ = place(t)
            push_or_keep(sq_out.at[strip(i)], sq0_in.at[p], SQ0, t, section=i // GROUPS)

        forward(0)
        all_here()
        spread(0)
        forward(1)
        spread(1)
        make_table()
        table_load.wait()

        @pl.when(early)
        def _():
            arrived(ENDS, pieces)

            def one(k, out):
                q = target(p, k)
                choose(0, pieces, q)
                push(picked.at[q, pl.ds(0, 2)], ins.at[pl.ds(2, 2), my_rows, my_cols], COT, 1, q, out)

            loop(EARLY, lambda k: one(k, COT))
            loop(N - EARLY, lambda k: one(k + EARLY, COT_LATE))
            loop(N, squashes)
            loop(N, norms)
            pl.semaphore_signal(go, inc=1, device_id={"section": 0, "peer": p + 1}, device_id_type=MESH)
            left(COT, picked.at[pl.ds(0, EARLY), pl.ds(0, 2)])

        @pl.when(late)
        def _():
            loop(N, squashes)
            pl.semaphore_wait(go, 1)
            arrived(ENDS, pieces)
            arrived(ENDH, pieces_h)

            def one(k):
                q = target(p, k)
                choose(0, pieces_h, q)
                choose(2, pieces, q)
                push(picked.at[q], ins.at[:, my_rows, my_cols], BOTH, 1, q)

            loop(N, one)
            scale()
            left(BOTH, picked)
            loop(N, norms)

        def up1():
            arrived(SQF, sqf)
            partial(small_u1, part_u, some_chunks(sqf), some_rows(pieces))
            send_up(small_u1, UPA1)

        def backward(stage):
            rows = pl.ds(pl.multiple_of(stage * PART, PART), PART)

            @pl.when((stage == 0) & early)
            def _():
                send_home(0)

            @pl.when(stage == 1)
            def _():
                @pl.when(early)
                def _():
                    up0()
                    up1()

            arrived(BND0 + stage, bnd.at[rows, :])
            gsq_ref[rows, :] = jnp.zeros((PART, RANK), F32)

            def into(t):
                cols = wide(t)
                gsq_ref[rows, :] += nt(bnd[rows, cols], up[:, cols])

            loop(WIDTH // WIDE, into)
            act = act_ref[rows, :]
            _, ga = middle(act, gsq_ref[rows, :])
            ga_out[rows, :] = ga

            def give(m):
                t = mate(p, stage, m)
                i, _ = place(t)
                push_or_keep(ga_out.at[strip(i)], ga0_in.at[p], GA0, t)

            loop(N // STAGES, give)
            inverse = inv_ref[rows, 0:1]
            dots = jnp.sum(ga.astype(F32) * act, axis=1, keepdims=True) * (1.0 / WIDTH)
            pull = inverse * inverse * dots

            def out(t):
                cols = wide(t)
                gn = nt(ga_out[rows, :], down[cols, :]) * gain_ref[0, :, cols].astype(F32)
                v = own[rows, cols].astype(F32)
                ends_v[rows, cols] = (bnd[rows, cols].astype(F32) + inverse * gn - v * pull).astype(BF)

            loop(WIDTH // WIDE, out)
            pltpu.make_async_copy(ends_v.at[rows, :], ends_ref.at[0, rows, :], load.at[ENDS_OUT + stage]).start()

        loop(STAGES, backward)

        arrived(NORM, norm_in)
        arrived(GA0, ga0_in)
        partial(small_d, part_d, some_rows(norm_in), some_rows(ga0_in))
        send_down(small_d, DOWN, 0)
        finish_up(UPA)

        @pl.when(late)
        def _():
            up1()
            down1()

        finish(DOWN)
        for stage in range(STAGES):
            half = pl.ds(stage * PART, PART)
            pltpu.make_async_copy(ends_v.at[half, :], ends_ref.at[0, half, :], load.at[ENDS_OUT + stage]).wait()
        left_but_own(DOWN, acc_d, my_j == p // WAYS)
        left(NORM, norm_in.at[pl.ds(0, N - 1)])
        left(GA0, ga0_in.at[pl.ds(0, N - 1)])
        left(UPA1, acc_u)

        @pl.when(early)
        def _():
            left(ENDH, pieces_h)
            left(SQ0, sq0_in.at[pl.ds(0, N - 1)])
            left(BND0, gathered.at[pl.ds(0, N - 1)])
            left(BND1, gathered)
            left(UPA, acc_u.at[pl.ds(0, WAYS - 1)])
            left(COT_LATE, picked.at[pl.ds(0, N - EARLY), pl.ds(0, 2)])

        @pl.when(late)
        def _():
            left(ENDH, pieces_h.at[pl.ds(0, N - 1)])
            left(SQ0, sq0_in)
            left(DOWN1, acc_d)

        left_chunks(early, WAYS - 1)

    @pl.when(second)
    def _():
        own_load.wait()
        all_here()

        def spread(stage):
            def one(m):
                t = mate(p, stage, m)
                i, j = place(t)
                push(own.at[strip(i), tile(j)], pieces.at[p], ENDS, 0, t)

            loop(N // STAGES, one)

        loop(STAGES, spread)
        for j in range(WAYS):
            for c in range(COLS // 128):
                at = COLS * j + 128 * c
                gain_out[j, c : c + 1, :] = gain_ref[0, :, at : at + 128].astype(F32)

        def gains(k):
            t = target(p, k)
            i, j = place(t)
            push_or_keep(gain_out.at[j], gain_in.at[p], GAIN, t, section=1 - i // GROUPS)

        loop(N, gains)
        down_load.wait()
        up_load.wait()
        make_table()
        table_load.wait()

        @pl.when(early)
        def _():
            arrived(ENDH, pieces_h)

            def one(k):
                q = target(p, k)
                choose(0, pieces_h, q)
                push_or_keep(
                    picked.at[q, pl.ds(0, 2)], ins.at[pl.ds(0, 2), my_rows, my_cols], HID, q
                )

            loop(N, one)
            scale()

        both = 2 * PART

        def through(stage):
            rows = pl.ds(pl.multiple_of(stage * PART, PART), PART)

            @pl.when(stage == 0)
            def _():
                arrived(HID, ins.at[pl.ds(0, 2), rows, :])
                arrived(COT, ins.at[pl.ds(2, 2), rows, :])

            @pl.when(stage == 1)
            def _():
                arrived(BOTH, ins.at[:, rows, :])

            squares = lax.fori_loop(
                0, WIDTH // WIDE,
                lambda t, c: c
                + jnp.sum(jnp.square(ins[0:2, rows, wide(t)].reshape(both, WIDE).astype(F32)), axis=1, keepdims=True),
                jnp.zeros((both, 1), F32),
            )
            inverse = lax.rsqrt(squares * (1.0 / WIDTH) + 1e-06)
            act_ref[0:both, :] = jnp.zeros((both, RANK), F32)

            def enter(t):
                cols = wide(t)
                v = ins[0:2, rows, cols].reshape(both, WIDE).astype(F32)
                n = (v * inverse * gain_ref[0, :, cols].astype(F32)).astype(BF)
                act_ref[0:both, :] += nn(n, down[cols, :])

            loop(WIDTH // WIDE, enter)
            gsq_ref[0:both, :] = jnp.zeros((both, RANK), F32)

            def into(t):
                cols = wide(t)
                gsq_ref[0:both, :] += nt(ins[2:4, rows, cols].reshape(both, WIDE), up[:, cols])

            loop(WIDTH // WIDE, into)
            act = act_ref[0:both, :]
            squashed, ga = middle(act, gsq_ref[0:both, :])
            sg_slots[:, rows, 0:RANK] = squashed.reshape(2, PART, RANK)
            ga32 = ga.astype(F32)
            sg_slots[:, rows, RANK : 2 * RANK] = (ga32 * inverse).astype(BF).reshape(2, PART, RANK)
            dots = jnp.sum(ga32 * act, axis=1, keepdims=True) * (1.0 / WIDTH)
            pull = inverse * inverse * dots

            def out(t):
                u = lax.rem(t + p + p // 4 + p // 16, WIDTH // WIDE)
                cols = wide(u)
                gn = nt(ga, down[cols, :]) * gain_ref[0, :, cols].astype(F32)
                v = ins[0:2, rows, cols].reshape(both, WIDE).astype(F32)
                c = ins[2:4, rows, cols].reshape(both, WIDE).astype(F32)
                ins[2:4, rows, cols] = (c + inverse * gn - v * pull).astype(BF).reshape(2, PART, WIDE)

                def give(n):
                    i = stage * GROUPS + lax.rem(n, GROUPS)
                    j = u * (WIDE // COLS) + n // GROUPS
                    push_or_keep(ins.at[pl.ds(2, 2), strip(i), tile(j)], back_in.at[pl.ds(2 * p, 2)], BACK, holder(i, j), section=stage)

                loop(GROUPS * WIDE // COLS, give)

            loop(WIDTH // WIDE, out)

            def extras(m):
                i = stage * GROUPS + lax.rem(m, GROUPS)
                c = m // GROUPS
                cols = pl.ds(pl.multiple_of(c * CHUNK, CHUNK), CHUNK)
                push_or_keep(sg_slots.at[:, strip(i), cols], sg_in.at[pl.ds(2 * p, 2)], SG, holder(i, 2 * c), section=stage)

            loop(GROUPS * (2 * RANK // CHUNK), extras)

        loop(STAGES, through)

        @pl.when(late)
        def _():
            send_home(1)

        pl.when(early)(down1)
        finish_up(UPA1)
        finish(DOWN1)
        arrived(BND1, ends_ref.at[0])
        left(ENDS, pieces)

        @pl.when(early)
        def _():
            left(GAIN, gain_in.at[pl.ds(0, N - 1)])
            left(BACK, back_in)
            left(HID, picked.at[pl.ds(0, N - 1), pl.ds(0, 2)])
            left_but_own(DOWN1, acc_d, my_j == p // WAYS)

        @pl.when(late)
        def _():
            left(GAIN, gain_in)
            left(BACK, back_in.at[pl.ds(0, 2 * N - 2)])
            left(BND0, gathered)
            left(BND1, gathered.at[pl.ds(0, N - 1)])
            left(UPA, acc_u)

        own_chunk = late & (lax.rem(my_j, 2) == 0)

        @pl.when(own_chunk)
        def _():
            left(SG, sg_in.at[pl.ds(0, N - 2)])

        @pl.when(jnp.logical_not(own_chunk))
        def _():
            left(SG, sg_in.at[pl.ds(0, N)])


        left_chunks(late, WAYS)


def shards(batch_ends, wiring, down_proj, up_proj, norm_gain):
    vmem = pl.BlockSpec(memory_space=pltpu.VMEM)
    hbm = pl.BlockSpec(memory_space=pl.ANY)
    block = (TOK, WIDTH)
    scratch = [
        pltpu.VMEM(block, BF),
        pltpu.VMEM((WIDTH, RANK), BF),
        pltpu.VMEM((RANK, WIDTH), BF),
        pltpu.VMEM((N, ROWS, COLS), BF),
        pltpu.VMEM((N, ROWS, COLS), BF),
        pltpu.VMEM((N, 4, ROWS, COLS), BF),
        pltpu.VMEM(block, BF),
        pltpu.VMEM(block, BF),
        pltpu.VMEM((4, *block), BF),
        pltpu.VMEM((WAYS, 8, 128), F32),
        pltpu.VMEM((N, 8, 128), F32),
        pltpu.VMEM((N, ROWS, COLS), BF),
        pltpu.VMEM((N, ROWS, COLS), BF),
        pltpu.VMEM((TOK, RANK), BF),
        pltpu.VMEM((N, ROWS, RANK), BF),
        pltpu.VMEM((2, TOK, 2 * RANK), BF),
        pltpu.VMEM((2 * N, ROWS, COLS), BF),
        pltpu.VMEM((2 * N, ROWS, CHUNK), BF),
        pltpu.VMEM((N, ROWS, CHUNK), BF),
        pltpu.VMEM((2, N, ROWS, CHUNK), BF),
        pltpu.VMEM((2, N, ROWS, CHUNK), BF),
        pltpu.VMEM((N, ROWS, COLS), BF),
        pltpu.VMEM(block, BF),
        pltpu.VMEM(block, BF),
        pltpu.VMEM((TOK, RANK), BF),
        pltpu.VMEM((N, ROWS, RANK), BF),
        pltpu.VMEM((2 * TOK, RANK), F32),
        pltpu.VMEM((2 * TOK, RANK), F32),
        pltpu.VMEM((TOK, 128), F32),
        pltpu.VMEM((COLS, RANK), F32),
        pltpu.VMEM((RANK, COLS), F32),
        pltpu.VMEM((COLS, RANK), BF),
        pltpu.VMEM((COLS, RANK), BF),
        pltpu.VMEM((RANK, COLS), BF),
        pltpu.VMEM((RANK, COLS), BF),
        pltpu.VMEM((WAYS, 80, RANK), BF),
        pltpu.VMEM((WAYS, 32, COLS), BF),
        pltpu.VMEM((WAYS, 8, COLS), F32),
        pltpu.VMEM((WAYS, 8, COLS), F32),
        pltpu.VMEM((N, 128), jnp.int32),
        pltpu.SMEM((N, 128), jnp.int32),
        pltpu.SemaphoreType.DMA((LOADS,)),
        pltpu.SemaphoreType.DMA((CLASSES,)),
        pltpu.SemaphoreType.DMA((CLASSES,)),
        pltpu.SemaphoreType.REGULAR,
    ]
    return pl.pallas_call(
        step_kernel,
        out_shape=(
            jax.ShapeDtypeStruct((1, *block), BF),
            jax.ShapeDtypeStruct((1, WIDTH // N, RANK), F32),
            jax.ShapeDtypeStruct((1, RANK // N, WIDTH), F32),
        ),
        in_specs=[vmem, vmem, hbm, hbm, hbm],
        out_specs=(hbm, vmem, vmem),
        scratch_shapes=scratch,
        compiler_params=pltpu.CompilerParams(
            collective_id=0, has_side_effects=True, vmem_limit_bytes=56 * 1024 * 1024
        ),
        name="adapter_step",
    )(wiring[None], norm_gain, batch_ends, down_proj, up_proj)


def solution(mesh):
    return jax.shard_map(
        shards,
        mesh=mesh,
        in_specs=(
            P("section", "peer", None),
            P(),
            P("section", "peer", None, None),
            P("section", "peer", None, None),
            P("section", "peer", None),
        ),
        out_specs=(
            P("section", "peer", None),
            P("section", "peer", None),
            P("section", "peer", None),
        ),
        check_vma=False,
    )
```
